32 devices in a mesh: row: 4 (over z), col: 8 (over y, x, core).
Axes of the slice: x: 2, y: 2, z: 4, core: 2. Of those that a mesh axis runs over, the one named last changes fastest.
Arguments:
- tiles: bfloat16 [4096, 128, 128], P(('row', 'col')), may hold values from -6 to 6
- tile_target: int32 [4096, 1], P(('row', 'col')), may hold values from 0 to 31; in each aligned block of 128 rows (0 to 127, 128 to 255, ...) at most 8 rows name the same one
- tile_place: int32 [4096], P(('row', 'col')), may hold values from 0 to 95
- density: bfloat16 [4096, 8192], P('col', 'row'), may hold values from -0.125 to 0.125
Outputs:
- contracted: bfloat16 [24576, 8192], P('col', 'row')
The draws below stay inside these ranges and needn't reach their ends.
Inputs may be any that keep to these rules, and one draw needn't show every extreme that they name: `tile_target`: among the tiles of one device, at most 8 name the same grid position, and some device has exactly 8 tiles for one position.
All inputs are finite; a program needn't handle non-finite values.
Results may differ from the reference program's by a relative error of at most 0.0046.
Values may be sent and summed in bfloat16 or wider, within the bound.
No kernel may reach another device: no remote copies, remote signals or barrier semaphores. Data moves between devices by JAX's collectives and lax.ppermute only.
A program may use at most 256 MiB of HBM per device.

```python
import math
import jax
import jax.numpy as jnp
import numpy as np
from jax import lax

BLOCK = 128
TILES_DEV = 128
ROW_BLOCKS_DEV = 24
K_BLOCKS = 4
COL_BLOCKS = 16
STEPS = 4
CAP = 8
POSITIONS = 96
TILES = 4096
SLAB_ROWS = 4096
OUT_COLS = 8192
N_ROW = 4
N_COL = 8
DEVICES = 32


def set_ends(entries, stream_key, smallest, top_value):
    spot = [jax.random.randint(jax.random.fold_in(stream_key, axis), (), 0, length) for axis, length in enumerate(entries.shape)]
    longest = entries.shape.index(max(entries.shape))
    beside = spot[:longest] + [(spot[longest] + 1) % entries.shape[longest]] + spot[longest + 1:]
    return entries.at[tuple(spot)].set(smallest).at[tuple(beside)].set(top_value)


def steps_of(own_key, extent, split, least, top_value):
    gain, own = 1.0, jax.random.fold_in(own_key, 6)
    for axis_at, parts in split:
        draws = jnp.exp(jax.random.uniform(jax.random.fold_in(own, axis_at), (parts,), jnp.float32, least / len(split), top_value / len(split)))
        gain = gain * jnp.repeat(draws, extent[axis_at] // parts).reshape([-1 if axis == axis_at else 1 for axis in range(len(extent))])
    return gain


def routed_block(key, own, number, rows, number_of, top, limit, lean):
    order = jax.random.permutation(key, number_of)
    crowded, usual = shares(number_of, rows * top, limit, lean, True), shares(number_of, rows * top, limit, lean, False)
    places = jnp.arange(number_of)

    def named(tallies, rotation):
        used = int((tallies > 0).sum())
        fixed = max(1, used // 4)
        shifted = fixed + (places - fixed + rotation * (used - fixed)) % max(1, number_of - fixed)
        return jnp.zeros((number_of,), jnp.int32).at[order[jnp.where(places < fixed, places, shifted)]].set(jnp.asarray(tallies, jnp.int32))

    tallies = jnp.where(number % 4 == 0, named(crowded, number // 4), named(usual, number - number // 4 - 1))
    mixed = jax.random.permutation(jax.random.fold_in(own, 3), number_of)
    giver, receiver = mixed[0:number_of // 2 * 2:2], mixed[1:number_of // 2 * 2:2]
    margin = jnp.minimum(tallies[giver] - 1, limit - tallies[receiver]) // 2
    margin = jnp.where((giver == order[0]) | (receiver == order[0]) | (tallies[receiver] == 0), 0, jnp.maximum(margin, 0))
    shifted = jax.random.randint(jax.random.fold_in(own, 4), (number_of // 2,), 0, 1 << 20) % (margin + 1)
    tallies = tallies.at[giver].add(-shifted).at[receiver].add(shifted)
    members = jnp.searchsorted(jnp.cumsum(tallies), jnp.arange(rows * top), side="right").astype(jnp.int32)
    listing = members.reshape(top, rows).T
    listing = listing[jax.random.permutation(jax.random.fold_in(own, 1), rows)]
    rotation = jax.random.randint(jax.random.fold_in(own, 2), (rows, 1), 0, top)
    return jnp.take_along_axis(listing, (jnp.arange(top)[None, :] + rotation) % top, axis=1)


def shares(amount, total, limit, lean, full):
    portions = [(1 << 20) // math.isqrt(standing ** lean) + 1 for standing in range(1, amount + 1)]
    largest = limit if full else min(limit, max(-(-total // amount), total * portions[0] // sum(portions)))
    least = 1 if total - largest >= amount - 1 else 0
    counts, spare = [largest] + [least] * (amount - 1), total - largest - least * (amount - 1)
    while spare > 0:
        movable = [i for i in range(1, amount) if counts[i] < largest] or [i for i in range(1, amount) if counts[i] < limit]
        mass, left = sum([portions[i] for i in movable]), spare
        for i in movable:
            extra = min(limit - counts[i], max(1, left * portions[i] // mass), spare)
            counts[i] = counts[i] + extra
            spare = spare - extra
    return np.array(counts)


def bell_draw(own_key, dims, spread, bound, split=(), held_as=jnp.bfloat16):
    loudness = steps_of(own_key, dims, split, -0.22, 0.18) if split else 1.0
    array = jax.random.normal(own_key, dims, jnp.float32) * spread * loudness
    return jnp.minimum(jnp.maximum(array, -bound), bound).astype(held_as)


def setup_inputs(seed: int = 0) -> dict:
    splits = jax.random.split(jax.random.key(seed), 5)
    tiles = bell_draw(splits[0], (TILES, BLOCK, BLOCK), 1.0, 6.0, ((0, 32),))
    tile_target_keys = jax.random.split(jax.random.fold_in(splits[1], 1), TILES // TILES_DEV)
    tile_target_turns = jax.random.permutation(jax.random.fold_in(splits[1], 3), TILES // TILES_DEV)
    tile_target = jax.vmap(lambda own, number: routed_block(jax.random.fold_in(splits[1], 2), own, number, TILES_DEV, DEVICES, 1, CAP, 2))(tile_target_keys, tile_target_turns).reshape((TILES, 1))
    tile_place = set_ends(jax.random.randint(splits[2], (TILES,), 0, POSITIONS), jax.random.fold_in(splits[2], 1), 0, POSITIONS - 1).astype(jnp.int32)
    density = bell_draw(splits[3], (SLAB_ROWS, OUT_COLS), (STEPS * K_BLOCKS * BLOCK) ** -0.5, 0.125, ((0, 8), (1, 4)))
    return dict(tiles=tiles, tile_target=tile_target, tile_place=tile_place, density=density)


def reference(tiles, tile_target, tile_place, density):
    tile_size = BLOCK
    segment_ids = (tile_target[:, 0] * POSITIONS + tile_place).astype(jnp.int32)
    summed = jax.ops.segment_sum(tiles.astype(jnp.float32), segment_ids, num_segments=DEVICES * POSITIONS)
    panels = summed.reshape(N_ROW, N_COL, ROW_BLOCKS_DEV, K_BLOCKS, tile_size, tile_size)
    panels = panels.transpose(0, 1, 2, 4, 3, 5).reshape(N_ROW, N_COL, ROW_BLOCKS_DEV * tile_size, K_BLOCKS * tile_size)
    panels = panels.astype(jnp.bfloat16)
    slabs = density.reshape(N_COL, K_BLOCKS * tile_size, N_ROW, COL_BLOCKS * tile_size).transpose(0, 2, 1, 3)

    def one_block(flat_index):
        row_index = flat_index // N_COL
        col_index = flat_index % N_COL
        total = jnp.zeros((ROW_BLOCKS_DEV * tile_size, COL_BLOCKS * tile_size), jnp.float32)
        for offset in range(STEPS):
            left = panels[(row_index + offset) % N_ROW, col_index]
            right = slabs[(col_index + offset) % N_COL, row_index]
            total = total + jnp.dot(left, right, preferred_element_type=jnp.float32)
        return total.astype(jnp.bfloat16)

    blocks = lax.map(one_block, jnp.arange(DEVICES, dtype=jnp.int32))
    blocks = blocks.reshape(N_ROW, N_COL, ROW_BLOCKS_DEV * tile_size, COL_BLOCKS * tile_size)
    return blocks.transpose(1, 2, 0, 3).reshape(N_COL * ROW_BLOCKS_DEV * tile_size, N_ROW * COL_BLOCKS * tile_size)
```

```python
import functools

import jax
import jax.numpy as jnp
from jax import lax
from jax.experimental import pallas as pl
from jax.experimental.pallas import tpu as pltpu
from jax.sharding import PartitionSpec as P

ROW_BLOCKS_DEV = 24
K_BLOCKS = 4
STEPS = 4
POSITIONS = 96

INWARD = [(0, 1), (3, 2)]
ACROSS = [(1, 2), (2, 1)]
OUTWARD = [(1, 0), (2, 3)]
LAG = 2
ROW_TILE = 4
VMEM_BYTES = 56 * 1024 * 1024


def passed_along(value, axis, steps):
    count = lax.axis_size(axis)
    pairs = [(source, (source + steps) % count) for source in range(count)]
    return lax.ppermute(value, axis, pairs)


def tile_capacity(tile_count, devices):
    return max(2, (2 * tile_count + devices - 1) // devices)


def ranks_of(targets):
    order = jnp.arange(targets.shape[0], dtype=jnp.int32)
    same_target = targets[:, None] == targets[None, :]
    earlier = order[None, :] < order[:, None]
    return jnp.sum((same_target & earlier).astype(jnp.int32), axis=1)


def on_device_ring(tiles, tile_target, tile_place, density):
    row_count = lax.axis_size("row")
    col_count = lax.axis_size("col")
    devices = row_count * col_count
    tile_count = tiles.shape[0]
    tile_size = tiles.shape[1]
    capacity = tile_capacity(tile_count, devices)
    slots = devices * capacity
    targets = tile_target[:, 0]
    order = jnp.arange(tile_count, dtype=jnp.int32)
    slot_of = targets * capacity + ranks_of(targets)
    hits = slot_of[None, :] == jnp.arange(slots, dtype=jnp.int32)[:, None]
    filled = jnp.any(hits, axis=1)
    source = jnp.sum(jnp.where(hits, order[None, :], 0), axis=1)
    send_tiles = jnp.take(tiles, source, axis=0)
    send_places = jnp.where(filled, jnp.take(tile_place, source), -1)
    got_tiles, got_places = (
        lax.all_to_all(send_tiles, ("row", "col"), split_axis=0, concat_axis=0, tiled=True),
        lax.all_to_all(send_places, ("row", "col"), split_axis=0, concat_axis=0, tiled=True),
    )
    got_tiles = got_tiles.reshape(slots, tile_size * tile_size)
    selector = (got_places[None, :] == jnp.arange(POSITIONS, dtype=jnp.int32)[:, None]).astype(
        jnp.bfloat16
    )
    dense = jnp.dot(selector, got_tiles, preferred_element_type=jnp.float32)
    dense = dense.reshape(ROW_BLOCKS_DEV, K_BLOCKS, tile_size, tile_size).transpose(0, 2, 1, 3)
    panel = dense.reshape(ROW_BLOCKS_DEV * tile_size, K_BLOCKS * tile_size).astype(jnp.bfloat16)
    total = jnp.zeros((panel.shape[0], density.shape[1]), jnp.float32)
    left, right = (panel, density)
    for offset in range(STEPS):
        total = total + jnp.dot(left, right, preferred_element_type=jnp.float32)
        if offset + 1 < STEPS:
            left = passed_along(left, "row", -1)
            right = passed_along(right, "col", -1)
    return total.astype(jnp.bfloat16)


def picked(tiles, source):
    count = source.shape[0]

    def kernel(source_ref, tiles_ref, out_ref, sem):
        def one(slot, carry):
            pltpu.make_async_copy(
                tiles_ref.at[source_ref[slot]], out_ref.at[slot], sem
            ).start()
            return carry

        lax.fori_loop(0, count, one, 0)
        pltpu.make_async_copy(tiles_ref.at[pl.ds(0, count)], out_ref, sem).wait()

    return pl.pallas_call(
        kernel,
        out_shape=jax.ShapeDtypeStruct((count,) + tiles.shape[1:], tiles.dtype),
        grid_spec=pltpu.PrefetchScalarGridSpec(
            num_scalar_prefetch=1,
            grid=(),
            in_specs=[pl.BlockSpec(memory_space=pl.ANY)],
            out_specs=pl.BlockSpec(memory_space=pl.ANY),
            scratch_shapes=[pltpu.SemaphoreType.DMA],
        ),
        name="pick_tiles",
    )(source, tiles)


def listed_sums(got, first_index, second_index, low, sizes):
    tile = got[0].shape[1:]
    slots = got[0].shape[0]
    entries = sum(sizes)
    parts = len(got)
    chunks = len(sizes)

    def kernel(first_ref, second_ref, *refs):
        got_refs = refs[:parts]
        out_refs = refs[parts : parts + 2 * chunks]
        total = refs[-1]
        for index_ref, outs in (
            (first_ref, out_refs[:chunks]),
            (second_ref, out_refs[chunks:]),
        ):

            def clear(entry, carry):
                total[entry] = jnp.zeros(tile, jnp.float32)
                return carry

            lax.fori_loop(0, entries, clear, 0)
            for part, got_ref in enumerate(got_refs):

                def add(slot, carry, part=part, got_ref=got_ref, index_ref=index_ref):
                    entry = index_ref[part * slots + slot] - low

                    @pl.when((entry >= 0) & (entry < entries))
                    def _():
                        total[entry] = total[entry] + got_ref[slot].astype(jnp.float32)

                    return carry

                lax.fori_loop(0, slots, add, 0)
            start = 0
            for size, out in zip(sizes, outs):

                def store(entry, carry, start=start, out=out):
                    out[entry] = total[start + entry].astype(out.dtype)
                    return carry

                lax.fori_loop(0, size, store, 0)
                start += size

    whole = pl.BlockSpec(memory_space=pltpu.VMEM)
    out = pl.pallas_call(
        kernel,
        out_shape=[jax.ShapeDtypeStruct((size,) + tile, got[0].dtype) for size in sizes] * 2,
        grid_spec=pltpu.PrefetchScalarGridSpec(
            num_scalar_prefetch=2,
            grid=(),
            in_specs=[whole] * parts,
            out_specs=[whole] * (2 * chunks),
            scratch_shapes=[pltpu.VMEM((entries,) + tile, jnp.float32)],
        ),
        compiler_params=pltpu.CompilerParams(vmem_limit_bytes=VMEM_BYTES),
        name="sum_tiles",
    )(first_index, second_index, *got)
    return list(out[:chunks]), list(out[chunks:])


def added(one, other):
    return (one.astype(jnp.float32) + other.astype(jnp.float32)).astype(one.dtype)


def chain_sums(first, second, token):
    count = len(first)
    near, inward, across, outward = {}, {}, {}, {}
    for step in range(count + 3 * LAG):
        sent, crossed, back, done = (step - lag * LAG for lag in range(4))
        held = {"token": token}
        if sent < count:
            held["sent"] = first[sent]
        if 0 <= crossed < count:
            held["inward"] = inward[crossed]
        if 0 <= back < count:
            held["across"] = across[back]
        if 0 <= done < count:
            held["outward"] = outward[done]
        held = lax.optimization_barrier(held)
        token = held["token"]
        if sent < count:
            inward[sent] = lax.ppermute(held["sent"], "row", INWARD)
        if 0 <= crossed < count:
            near[crossed] = added(first[crossed], held["inward"])
            across[crossed] = lax.ppermute(near[crossed], "row", ACROSS)
            token = near[crossed]
        if 0 <= back < count:
            across[back] = held["across"]
            outward[back] = lax.ppermute(added(second[back], held["across"]), "row", OUTWARD)
        if 0 <= done < count:
            outward[done] = held["outward"]
    in_order = [[part[step] for step in range(count)] for part in (near, across, outward)]
    return in_order, token


def contracted_rows(rows, at_end, first_at, second_at, slabs, chunks, low, before, out_dtype):
    near, across, outward = chunks
    sizes = [chunk.shape[0] for chunk in near]
    entries = sum(sizes)
    tile = near[0].shape[1]
    count = len(near)
    depth = K_BLOCKS * tile
    columns = slabs[0].shape[1]
    row_count = len(slabs)
    panels = len(rows)
    block = (ROW_TILE * tile, columns)
    col_tile = min(512, columns)

    def kernel(place_ref, first_ref, second_ref, *refs):
        near_refs, across_refs, outward_refs = (
            refs[part * count : (part + 1) * count] for part in range(3)
        )
        refs = refs[3 * count :]
        slab_refs = refs[:row_count]
        refs = refs[row_count:]
        if before is not None:
            before_ref, refs = refs[0], refs[1:]
        out_ref, near_held, far_held, slab_held, left, sems = refs
        step = pl.program_id(0)
        me, end = place_ref[0], place_ref[1]

        @pl.when(step == 0)
        def _():
            start = 0
            for part in range(count):
                there = pl.ds(start, sizes[part])
                pltpu.make_async_copy(
                    near_refs[part], near_held.at[there], sems.at[2 * part]
                ).start()

                @pl.when(end == 1)
                def _():
                    pltpu.make_async_copy(
                        outward_refs[part], far_held.at[there], sems.at[2 * part + 1]
                    ).start()

                @pl.when(end == 0)
                def _():
                    pltpu.make_async_copy(
                        across_refs[part], far_held.at[there], sems.at[2 * part + 1]
                    ).start()

                start += sizes[part]
            for at, row in enumerate(rows):
                offset = lax.rem(row - me + row_count, row_count)
                for which in range(row_count):

                    @pl.when(offset == which)
                    def _():
                        pltpu.make_async_copy(
                            slab_refs[which],
                            slab_held.at[pl.ds(at * depth, depth)],
                            sems.at[2 * count + at],
                        ).start()

            near_held[entries] = jnp.zeros((tile, tile), near_held.dtype)
            far_held[entries] = jnp.zeros((tile, tile), far_held.dtype)
            start = 0
            for part in range(count):
                there = pl.ds(start, sizes[part])
                pltpu.make_async_copy(
                    near_refs[part], near_held.at[there], sems.at[2 * part]
                ).wait()
                pltpu.make_async_copy(
                    near_refs[part], far_held.at[there], sems.at[2 * part + 1]
                ).wait()
                start += sizes[part]
            for at in range(panels):
                pltpu.make_async_copy(
                    slab_refs[0],
                    slab_held.at[pl.ds(at * depth, depth)],
                    sems.at[2 * count + at],
                ).wait()

        def fill(row_block, carry):
            for at, row in enumerate(rows):
                for k in range(K_BLOCKS):
                    place = row * POSITIONS + (step * ROW_TILE + row_block) * K_BLOCKS + k
                    one = jnp.minimum(first_ref[place] - low, entries)
                    other = jnp.minimum(second_ref[place] - low, entries)
                    left[
                        pl.ds(pl.multiple_of(row_block * tile, tile), tile),
                        (at * K_BLOCKS + k) * tile : (at * K_BLOCKS + k + 1) * tile,
                    ] = added(near_held[one], far_held[other])
            return carry

        lax.fori_loop(0, ROW_TILE, fill, 0)
        for column in range(0, columns, col_tile):
            part = slice(column, column + col_tile)
            product = jnp.dot(
                left[...], slab_held[:, part], preferred_element_type=jnp.float32
            )
            if before is not None:
                product = product + before_ref[:, part]
            out_ref[:, part] = product.astype(out_ref.dtype)

    anywhere = pl.BlockSpec(memory_space=pl.ANY)
    blocked = pl.BlockSpec(block, lambda step, *_: (step, 0))
    extra = () if before is None else (before,)
    place = jnp.stack([lax.axis_index("row"), at_end]).astype(jnp.int32)
    return pl.pallas_call(
        kernel,
        out_shape=jax.ShapeDtypeStruct((ROW_BLOCKS_DEV * tile, columns), out_dtype),
        grid_spec=pltpu.PrefetchScalarGridSpec(
            num_scalar_prefetch=3,
            grid=(ROW_BLOCKS_DEV // ROW_TILE,),
            in_specs=[anywhere] * (3 * count + row_count) + [blocked] * len(extra),
            out_specs=blocked,
            scratch_shapes=[
                pltpu.VMEM((entries + 1, tile, tile), near[0].dtype),
                pltpu.VMEM((entries + 1, tile, tile), near[0].dtype),
                pltpu.VMEM((panels * depth, columns), slabs[0].dtype),
                pltpu.VMEM((ROW_TILE * tile, panels * depth), near[0].dtype),
                pltpu.SemaphoreType.DMA((2 * count + panels,)),
            ],
        ),
        compiler_params=pltpu.CompilerParams(vmem_limit_bytes=VMEM_BYTES),
        cost_estimate=pl.CostEstimate(
            flops=2 * ROW_BLOCKS_DEV * tile * panels * depth * columns,
            bytes_accessed=2 * entries * tile * tile * 2,
            transcendentals=0,
        ),
        name="contract_panels",
    )(place, first_at, second_at, *near, *across, *outward, *slabs, *extra)


def on_device_chain(tiles, tile_target, tile_place, density):
    row_count = lax.axis_size("row")
    col_count = lax.axis_size("col")
    devices = row_count * col_count
    tile_count, tile_size = tiles.shape[:2]
    capacity = tile_capacity(tile_count, devices)
    plane_slots = col_count * capacity
    all_entries = row_count * POSITIONS
    me = lax.axis_index("row")
    column = lax.axis_index("col")
    at_end = ((me == 0) | (me == row_count - 1)).astype(jnp.int32)

    targets = tile_target[:, 0]
    order = jnp.arange(tile_count, dtype=jnp.int32)
    slot_of = targets * capacity + ranks_of(targets)
    hits = slot_of[None, :] == jnp.arange(devices * capacity, dtype=jnp.int32)[:, None]
    source = jnp.sum(jnp.where(hits, order[None, :], 0), axis=1).reshape(row_count, plane_slots)
    codes = lax.all_gather(slot_of * POSITIONS + tile_place, ("row", "col"), tiled=True)
    got = []
    for row in range(row_count):
        sent = picked(tiles, source[row])
        if got:
            sent, got[-1] = lax.optimization_barrier((sent, got[-1]))
        got.append(lax.all_to_all(sent, "col", split_axis=0, concat_axis=0, tiled=True))

    slabs = [density]
    density, got[2] = lax.optimization_barrier((density, got[2]))
    for offset in range(1, STEPS):
        slabs.append(passed_along(slabs[-1] if offset > 1 else density, "col", -1))

    codes = codes.reshape(row_count, col_count * tile_count)
    code_target = codes // (POSITIONS * capacity)
    code_place = codes % POSITIONS
    by_target = (code_target[:, None, :] == jnp.arange(devices, dtype=jnp.int32)[None, :, None])
    by_place = (code_place[:, None, :] == jnp.arange(POSITIONS, dtype=jnp.int32)[None, :, None])
    held = jnp.einsum(
        "ptn,pqn->ptq",
        by_target.astype(jnp.bfloat16),
        by_place.astype(jnp.bfloat16),
        preferred_element_type=jnp.float32,
    )
    rightward = jnp.sum(held[: row_count - 1], axis=0) > 0
    leftward = jnp.sum(held[1:], axis=0) > 0
    used = jnp.stack([rightward, leftward]).astype(jnp.int32)
    used = used.reshape(2, row_count, col_count, POSITIONS)
    tallies = jnp.sum(used, axis=3)
    earliest = [row * (POSITIONS // 2) for row in range(row_count)]
    starts, end = [], jnp.zeros((2, col_count), jnp.int32)
    for row in range(row_count):
        starts.append(jnp.maximum(end, earliest[row]))
        end = starts[-1] + tallies[:, row]
    needed = jnp.max(end)
    starts = jnp.stack(starts, axis=1)
    mine = lax.dynamic_index_in_dim(used, column, 2, keepdims=False)
    my_starts = lax.dynamic_index_in_dim(starts, column, 2, keepdims=False)
    before_it = jnp.arange(POSITIONS)[:, None] < jnp.arange(POSITIONS)[None, :]
    earlier = jnp.sum(jnp.where(before_it[None, None], mine[..., None], 0), axis=2)
    listed = jnp.where(mine > 0, my_starts[..., None] + earlier, all_entries)
    is_low = me < row_count // 2
    first_at = jnp.where(is_low, listed[0], listed[1])
    second_at = jnp.where(is_low, listed[1], listed[0])

    near_codes = lax.dynamic_index_in_dim(codes, me, 0, keepdims=False)
    near_codes = near_codes.reshape(col_count, 1, tile_count)
    wanted = jnp.arange(row_count, dtype=jnp.int32)[:, None] * col_count + column
    wanted = (wanted * capacity + jnp.arange(capacity, dtype=jnp.int32)[None, :]).reshape(1, -1, 1)
    found = (near_codes // POSITIONS) == wanted
    got_place = jnp.sum(jnp.where(found, near_codes % POSITIONS + 1, 0), axis=2) - 1
    got_place = got_place.reshape(col_count, row_count, capacity).transpose(1, 0, 2)
    got_place = got_place.reshape(row_count, plane_slots, 1)
    at_place = got_place == jnp.arange(POSITIONS, dtype=jnp.int32)[None, None, :]

    def entries_of(table):
        entry = jnp.sum(jnp.where(at_place, table[:, None, :] + 1, 0), axis=2) - 1
        return entry.reshape(-1)

    first_index, second_index = entries_of(first_at), entries_of(second_at)
    first_at, second_at = first_at.reshape(-1), second_at.reshape(-1)

    segments = [
        (1, [8, 8, 16, 16]),
        (2, [16, 16, 16]),
        (3, [16, 16, 16]),
        (4, [16] * 5),
        (4, [16] * 4 + [8, 4, 4]),
    ]
    low = 0
    first, second = [], []
    for parts, sizes in segments:
        one, other = listed_sums(got[:parts], first_index, second_index, low, sizes)
        first += one
        second += other
        low += sum(sizes)
    main_entries = low
    chunks, token = chain_sums(first, second, first_index)

    half = row_count // 2
    sizes = [chunk.shape[0] for chunk in first]
    bounds = [sum(sizes[:at]) for at in range(len(sizes) + 1)]
    early = bounds.index(half * POSITIONS)
    late = bounds.index(earliest[half])
    early_rows, late_rows = tuple(range(half)), tuple(range(half, row_count))
    common = (at_end, first_at, second_at, slabs)
    partial = contracted_rows(
        early_rows, *common, [part[:early] for part in chunks], 0, None, jnp.float32
    )
    chunks = [part[late:] for part in chunks]

    def finish(near, across, outward):
        return contracted_rows(
            late_rows, *common, (near, across, outward), earliest[half], partial, density.dtype
        )

    def with_rest(near, across, outward):
        rest = all_entries - main_entries
        sizes = [16] * (rest // 16 - 1) + [8, 8]
        one, other = listed_sums(got, first_index, second_index, main_entries, sizes)
        more, _ = chain_sums(one, other, first_index)
        return finish(near + more[0], across + more[1], outward + more[2])

    return lax.cond(needed <= main_entries, finish, with_rest, *chunks)


def solution(mesh):
    in_specs = (
        P(("row", "col"), None, None),
        P(("row", "col"), None),
        P(("row", "col")),
        P("col", "row"),
    )
    out_specs = P("col", "row")
    on_device = on_device_chain if mesh.shape["row"] == STEPS else on_device_ring
    return jax.shard_map(
        on_device, mesh=mesh, in_specs=in_specs, out_specs=out_specs, check_vma=False
    )
```

```python
import functools

import jax
import jax.numpy as jnp
from jax import lax
from jax.experimental import pallas as pl
from jax.experimental.pallas import tpu as pltpu
from jax.sharding import PartitionSpec as P

ROW_BLOCKS_DEV = 24
K_BLOCKS = 4
STEPS = 4
POSITIONS = 96

INWARD = [(0, 1), (3, 2)]
ACROSS = [(1, 2), (2, 1)]
OUTWARD = [(1, 0), (2, 3)]
LAG = 2

CHUNK = 24
ALONE, ONE_BEFORE, FIRST_PAIR, LAST_PAIR = 24, 72, 120, 192
LIST_ENTRIES = FIRST_PAIR + LAST_PAIR
NOWHERE = 1 << 15
ROW_TILE = 4
SUM_VMEM_BYTES = 56 * 1024 * 1024
CONTRACT_VMEM_BYTES = 44 * 1024 * 1024
SMALL = pl.CostEstimate(flops=1000, bytes_accessed=1000, transcendentals=0)


def passed_along(value, axis, steps):
    count = lax.axis_size(axis)
    pairs = [(source, (source + steps) % count) for source in range(count)]
    return lax.ppermute(value, axis, pairs)


def tile_capacity(tile_count, devices):
    return max(2, (2 * tile_count + devices - 1) // devices)


def ranks_of(targets):
    order = jnp.arange(targets.shape[0], dtype=jnp.int32)
    same_target = targets[:, None] == targets[None, :]
    earlier = order[None, :] < order[:, None]
    return jnp.sum((same_target & earlier).astype(jnp.int32), axis=1)


def on_device_ring(tiles, tile_target, tile_place, density):
    row_count = lax.axis_size("row")
    col_count = lax.axis_size("col")
    devices = row_count * col_count
    tile_count = tiles.shape[0]
    tile_size = tiles.shape[1]
    capacity = tile_capacity(tile_count, devices)
    slots = devices * capacity
    targets = tile_target[:, 0]
    order = jnp.arange(tile_count, dtype=jnp.int32)
    slot_of = targets * capacity + ranks_of(targets)
    hits = slot_of[None, :] == jnp.arange(slots, dtype=jnp.int32)[:, None]
    filled = jnp.any(hits, axis=1)
    source = jnp.sum(jnp.where(hits, order[None, :], 0), axis=1)
    send_tiles = jnp.take(tiles, source, axis=0)
    send_places = jnp.where(filled, jnp.take(tile_place, source), -1)
    got_tiles, got_places = (
        lax.all_to_all(send_tiles, ("row", "col"), split_axis=0, concat_axis=0, tiled=True),
        lax.all_to_all(send_places, ("row", "col"), split_axis=0, concat_axis=0, tiled=True),
    )
    got_tiles = got_tiles.reshape(slots, tile_size * tile_size)
    selector = (got_places[None, :] == jnp.arange(POSITIONS, dtype=jnp.int32)[:, None]).astype(
        jnp.bfloat16
    )
    dense = jnp.dot(selector, got_tiles, preferred_element_type=jnp.float32)
    dense = dense.reshape(ROW_BLOCKS_DEV, K_BLOCKS, tile_size, tile_size).transpose(0, 2, 1, 3)
    panel = dense.reshape(ROW_BLOCKS_DEV * tile_size, K_BLOCKS * tile_size).astype(jnp.bfloat16)
    total = jnp.zeros((panel.shape[0], density.shape[1]), jnp.float32)
    left, right = (panel, density)
    for offset in range(STEPS):
        total = total + jnp.dot(left, right, preferred_element_type=jnp.float32)
        if offset + 1 < STEPS:
            left = passed_along(left, "row", -1)
            right = passed_along(right, "col", -1)
    return total.astype(jnp.bfloat16)


def picked(tiles, source):
    count = source.shape[0]

    def kernel(source_ref, tiles_ref, out_ref):
        def one(slot, carry):
            out_ref[slot] = tiles_ref[source_ref[slot]]
            return carry

        lax.fori_loop(0, count, one, 0, unroll=4)

    return pl.pallas_call(
        kernel,
        out_shape=jax.ShapeDtypeStruct((count,) + tiles.shape[1:], tiles.dtype),
        grid_spec=pltpu.PrefetchScalarGridSpec(
            num_scalar_prefetch=1,
            grid=(),
            in_specs=[pl.BlockSpec(memory_space=pltpu.VMEM)],
            out_specs=pl.BlockSpec(memory_space=pltpu.VMEM),
        ),
        compiler_params=pltpu.CompilerParams(vmem_limit_bytes=SUM_VMEM_BYTES),
        cost_estimate=SMALL,
        name="pick_tiles",
    )(source, tiles)


def hops_before(chunk):
    at = chunk * CHUNK
    at = at if at < FIRST_PAIR else at - FIRST_PAIR
    return 0 if at < ALONE else 1 if at < ONE_BEFORE else 2


def listed_sums(got, order, bounds, wanted, after):
    tile = got[0].shape[1:]
    slots = got[0].shape[0]
    parts = len(got)
    count = len(wanted)

    def kernel(order_ref, bounds_ref, *refs):
        got_refs, out_refs = refs[:parts], refs[-2 - count : -2]
        held, sems = refs[-2:]
        copies = [
            pltpu.make_async_copy(got_ref, held.at[pl.ds(part * slots, slots)], sems.at[part])
            for part, got_ref in enumerate(got_refs)
        ]
        for copy in copies:
            copy.start()
        for copy in copies:
            copy.wait()
        for (which, chunk), out in zip(wanted, out_refs):

            def total(entry, carry, which=which, chunk=chunk, out=out):
                def add(at, value):
                    return value + held[order_ref[which, at]].astype(jnp.float32)

                at = chunk * CHUNK + entry
                value = lax.fori_loop(
                    bounds_ref[which, at],
                    bounds_ref[which, at + 1],
                    add,
                    jnp.zeros(tile, jnp.float32),
                )
                out[entry] = value.astype(out.dtype)
                return carry

            lax.fori_loop(0, CHUNK, total, 0)

    out = pl.pallas_call(
        kernel,
        out_shape=[jax.ShapeDtypeStruct((CHUNK,) + tile, got[0].dtype)] * count,
        grid_spec=pltpu.PrefetchScalarGridSpec(
            num_scalar_prefetch=2,
            grid=(),
            in_specs=[pl.BlockSpec(memory_space=pl.ANY)] * (parts + len(after)),
            out_specs=[pl.BlockSpec(memory_space=pltpu.VMEM)] * count,
            scratch_shapes=[
                pltpu.VMEM((parts * slots,) + tile, got[0].dtype),
                pltpu.SemaphoreType.DMA((parts,)),
            ],
        ),
        compiler_params=pltpu.CompilerParams(vmem_limit_bytes=SUM_VMEM_BYTES),
        cost_estimate=SMALL,
        name="sum_tiles",
    )(order, bounds, *got, *after)
    return dict(zip(wanted, out))


def added(one, other, after):
    def kernel(one_ref, other_ref, *refs):
        out_ref = refs[-1]

        def add(entry, carry):
            out_ref[entry] = one_ref[entry] + other_ref[entry]
            return carry

        lax.fori_loop(0, one.shape[0], add, 0, unroll=4)

    held = pl.BlockSpec(memory_space=pltpu.VMEM)
    return pl.pallas_call(
        kernel,
        out_shape=jax.ShapeDtypeStruct(one.shape, one.dtype),
        in_specs=[held, held] + [pl.BlockSpec(memory_space=pl.ANY)] * len(after),
        out_specs=held,
        compiler_params=pltpu.CompilerParams(vmem_limit_bytes=SUM_VMEM_BYTES),
        cost_estimate=SMALL,
        name="add_tiles",
    )(one, other, *after)


def chain_sums(sums_of, groups, slabs):
    count = LIST_ENTRIES // CHUNK
    pair_at = FIRST_PAIR // CHUNK
    near, inward, across, outward = {}, {}, {}, {}
    listed = {}
    last = None

    def sums(group):
        nonlocal last
        listed.update(sums_of(group, [] if last is None else [last]))
        last = listed[group[0]]

    def summed(one, other, after):
        nonlocal last
        last = added(one, other, [last] + after)
        return last

    def enter(chunk):
        if chunk < count and hops_before(chunk) == 2:
            inward[chunk] = lax.ppermute(listed[0, chunk], "row", INWARD)

    def cross(chunk):
        if chunk < count and hops_before(chunk):
            near[chunk] = listed[0, chunk]
            if hops_before(chunk) == 2:
                near[chunk] = summed(near[chunk], inward[chunk], [])
            across[chunk] = lax.ppermute(near[chunk], "row", ACROSS)

    def leave(chunk):
        moving = listed[1, chunk]
        if hops_before(chunk):
            after = [outward[chunk - LAG]] if chunk >= LAG else []
            if chunk > pair_at and (chunk - pair_at) % 2 == 0:
                after += slabs[(chunk - pair_at) // 2 :][:1]
            moving = summed(moving, across[chunk], after)
        outward[chunk] = lax.ppermute(moving, "row", OUTWARD)

    sums(groups[0])
    leave(0)
    cross(1)
    enter(3)
    sums(groups[1])
    cross(2)
    enter(4)
    for chunk in range(1, count):
        leave(chunk)
        cross(chunk + LAG)
        if chunk > 1 and chunk in groups:
            sums(groups[chunk])
        enter(chunk + 2 * LAG)
    return near, across, outward


def contracted(place, first_at, second_at, slabs, chunks):
    near, across, outward = chunks
    count = len(outward)
    entries = count * CHUNK
    tile = outward[0].shape[1]
    depth = K_BLOCKS * tile
    columns = slabs[0].shape[1]
    row_count = len(slabs)
    steps = ROW_BLOCKS_DEV // ROW_TILE
    col_tile = min(512, columns)
    both = sorted(near)

    def kernel(place_ref, first_ref, second_ref, *refs):
        near_refs = dict(zip(both, refs))
        across_refs = dict(zip(both, refs[len(both) :]))
        outward_refs = refs[2 * len(both) : 2 * len(both) + count]
        slab_refs = refs[2 * len(both) + count : 2 * len(both) + count + row_count]
        out_ref, near_held, far_held, slab_held, left, sems = refs[-6:]
        step = pl.program_id(0)
        me, end = place_ref[0], place_ref[1]

        @pl.when(step == 0)
        def _():
            for part in range(count):
                there = pl.ds(part * CHUNK, CHUNK)

                def from_outward(part=part, there=there):
                    pltpu.make_async_copy(
                        outward_refs[part], far_held.at[there], sems.at[2 * part + 1]
                    ).start()

                if part not in near_refs:
                    from_outward()
                    continue
                pltpu.make_async_copy(
                    near_refs[part], near_held.at[there], sems.at[2 * part]
                ).start()
                pl.when(end == 1)(from_outward)

                @pl.when(end == 0)
                def _(part=part, there=there):
                    pltpu.make_async_copy(
                        across_refs[part], far_held.at[there], sems.at[2 * part + 1]
                    ).start()

            for row in range(row_count):
                offset = lax.rem(row - me + row_count, row_count)
                for which in range(row_count):

                    @pl.when(offset == which)
                    def _(row=row, which=which):
                        pltpu.make_async_copy(
                            slab_refs[which],
                            slab_held.at[pl.ds(row * depth, depth)],
                            sems.at[2 * count + row],
                        ).start()

            near_held[entries] = jnp.zeros((tile, tile), near_held.dtype)
            far_held[entries] = jnp.zeros((tile, tile), far_held.dtype)
            for part in range(count):
                there = pl.ds(part * CHUNK, CHUNK)
                if part in near_refs:
                    pltpu.make_async_copy(
                        near_refs[part], near_held.at[there], sems.at[2 * part]
                    ).wait()
                pltpu.make_async_copy(
                    outward_refs[part], far_held.at[there], sems.at[2 * part + 1]
                ).wait()
            for row in range(row_count):
                pltpu.make_async_copy(
                    slab_refs[0],
                    slab_held.at[pl.ds(row * depth, depth)],
                    sems.at[2 * count + row],
                ).wait()

        def fill(row_block, carry):
            for row in range(row_count):
                for k in range(K_BLOCKS):
                    at = row * POSITIONS + (step * ROW_TILE + row_block) * K_BLOCKS + k
                    one = jnp.minimum(first_ref[at], entries)
                    other = jnp.minimum(second_ref[at], entries)
                    there = (row * K_BLOCKS + k) * tile
                    left[
                        pl.ds(pl.multiple_of(row_block * tile, tile), tile),
                        there : there + tile,
                    ] = near_held[one] + far_held[other]
            return carry

        lax.fori_loop(0, ROW_TILE, fill, 0)
        for column in range(0, columns, col_tile):
            part = slice(column, column + col_tile)
            out_ref[:, part] = jnp.dot(
                left[...], slab_held[:, part], preferred_element_type=jnp.float32
            ).astype(out_ref.dtype)

    anywhere = pl.BlockSpec(memory_space=pl.ANY)
    operands = (place, first_at, second_at)
    operands += tuple(near[part] for part in both) + tuple(across[part] for part in both)
    operands += tuple(outward[part] for part in range(count)) + tuple(slabs)
    return pl.pallas_call(
        kernel,
        out_shape=jax.ShapeDtypeStruct((ROW_BLOCKS_DEV * tile, columns), slabs[0].dtype),
        grid_spec=pltpu.PrefetchScalarGridSpec(
            num_scalar_prefetch=3,
            grid=(steps,),
            in_specs=[anywhere] * (len(operands) - 3),
            out_specs=pl.BlockSpec((ROW_TILE * tile, columns), lambda step, *_: (step, 0)),
            scratch_shapes=[
                pltpu.VMEM((entries + 1, tile, tile), slabs[0].dtype),
                pltpu.VMEM((entries + 1, tile, tile), slabs[0].dtype),
                pltpu.VMEM((row_count * depth, columns), slabs[0].dtype),
                pltpu.VMEM((ROW_TILE * tile, row_count * depth), slabs[0].dtype),
                pltpu.SemaphoreType.DMA((2 * count + row_count,)),
            ],
        ),
        compiler_params=pltpu.CompilerParams(vmem_limit_bytes=CONTRACT_VMEM_BYTES),
        cost_estimate=SMALL,
        name="contract_panels",
    )(*operands)


def on_device_chain(tiles, tile_target, tile_place, density):
    row_count = lax.axis_size("row")
    col_count = lax.axis_size("col")
    devices = row_count * col_count
    tile_count, tile_size = tiles.shape[:2]
    capacity = tile_capacity(tile_count, devices)
    plane_slots = col_count * capacity
    me = lax.axis_index("row")
    column = lax.axis_index("col")
    at_end = ((me == 0) | (me == row_count - 1)).astype(jnp.int32)

    targets = tile_target[:, 0]
    codes = jnp.broadcast_to(targets * POSITIONS + tile_place, (devices, tile_count))
    codes = lax.all_to_all(codes, ("row", "col"), split_axis=0, concat_axis=0, tiled=True)
    order = jnp.arange(tile_count, dtype=jnp.int32)
    slot_of = targets * capacity + ranks_of(targets)
    hits = slot_of[None, :] == jnp.arange(devices * capacity, dtype=jnp.int32)[:, None]
    source = jnp.sum(jnp.where(hits, order[None, :], 0), axis=1)

    def exchanged(chosen):
        return lax.all_to_all(chosen, "col", split_axis=0, concat_axis=0, tiled=True)

    half = row_count // 2
    source = source.reshape(2, half, col_count, capacity)
    source = source.transpose(0, 2, 1, 3).reshape(2, half * plane_slots)

    def sent_half(which):
        return picked(tiles, source[which])

    got = [exchanged(sent_half(0))]
    codes = codes.reshape(row_count, col_count * tile_count)
    code_target = codes // POSITIONS
    code_place = codes % POSITIONS
    by_target = (code_target[:, None, :] == jnp.arange(devices, dtype=jnp.int32)[None, :, None])
    by_place = (code_place[:, None, :] == jnp.arange(POSITIONS, dtype=jnp.int32)[None, :, None])
    held = jnp.einsum(
        "ptn,pqn->ptq",
        by_target.astype(jnp.bfloat16),
        by_place.astype(jnp.bfloat16),
        preferred_element_type=jnp.float32,
    )
    filled = held > 0
    classes = jnp.stack(
        [
            jnp.stack([~filled[a] & ~filled[b] & filled[c], ~filled[a] & filled[b], filled[a]])
            for a, b, c in ((0, 1, 2), (3, 2, 1))
        ]
    ).astype(jnp.int32)
    classes = classes.reshape(2, 3, 2, half, col_count, POSITIONS)
    counts = jnp.sum(classes, axis=(3, 5))
    begin = jnp.maximum(counts[:, 0, 0], ALONE)
    last_first = jnp.maximum(begin + counts[:, 1, 0], ONE_BEFORE)
    over = jnp.maximum(last_first + counts[:, 2, 0] - FIRST_PAIR, 0)
    later = jnp.maximum(counts[:, 0, 1], ALONE) + FIRST_PAIR
    last = jnp.maximum(later + counts[:, 1, 1], FIRST_PAIR + ONE_BEFORE)
    fits = (last_first <= FIRST_PAIR) & (last + over + counts[:, 2, 1] <= LIST_ENTRIES)
    fits = jnp.all(fits)
    zero = jnp.zeros_like(begin)
    starts = jnp.stack(
        [zero, begin, last_first, zero + FIRST_PAIR, later, last + over, last], axis=1
    )
    starts = lax.dynamic_index_in_dim(starts, column, 2, keepdims=False)
    mine = lax.dynamic_index_in_dim(classes, column, 4, keepdims=False)
    mine = mine.reshape(2, 3, 2, half * POSITIONS)
    spot = jnp.arange(half * POSITIONS, dtype=jnp.int32)
    before_it = spot[:, None] < spot[None, :]
    rank = jnp.sum(jnp.where(before_it, mine[..., None], 0), axis=3)
    at = rank + starts[:, :6].reshape(2, 2, 3).transpose(0, 2, 1)[..., None]
    moved = at - FIRST_PAIR + starts[:, 6][:, None, None, None]
    first_pair = jnp.arange(2)[None, None, :, None] == 0
    at = jnp.where(first_pair & (at >= FIRST_PAIR), moved, at)
    listed = jnp.min(jnp.where(mine > 0, at, NOWHERE), axis=1)
    listed = listed.reshape(2, row_count, POSITIONS)
    is_low = me < row_count // 2
    first_at = jnp.where(is_low, listed[0], listed[1])
    second_at = jnp.where(is_low, listed[1], listed[0])

    near_codes = lax.dynamic_index_in_dim(codes, me, 0, keepdims=False)
    near_codes = near_codes.reshape(col_count, tile_count)
    near_targets = near_codes // POSITIONS
    near_slots = (near_targets * capacity + jax.vmap(ranks_of)(near_targets))[:, None, :]
    near_places = (near_codes % POSITIONS)[:, None, :]
    wanted = jnp.arange(row_count, dtype=jnp.int32)[:, None] * col_count + column
    wanted = (wanted * capacity + jnp.arange(capacity, dtype=jnp.int32)[None, :]).reshape(1, -1, 1)
    got_place = jnp.sum(jnp.where(near_slots == wanted, near_places + 1, 0), axis=2) - 1
    got_place = got_place.reshape(col_count, row_count, capacity).transpose(1, 0, 2)
    got_place = got_place.reshape(row_count, plane_slots, 1)
    at_place = got_place == jnp.arange(POSITIONS, dtype=jnp.int32)[None, None, :]

    def entries_of(table):
        entry = jnp.sum(jnp.where(at_place, table[:, None, :] + 1, 0), axis=2) - 1
        entry = jnp.where(got_place[..., 0] < 0, NOWHERE, entry)
        entry = entry.reshape(2, half, col_count, capacity)
        return entry.transpose(0, 2, 1, 3).reshape(-1)

    entry = jnp.stack([entries_of(first_at), entries_of(second_at)])
    slot = jnp.arange(row_count * plane_slots, dtype=jnp.int32)
    one, other = entry[:, :, None], entry[:, None, :]
    ahead = (other < one) | ((other == one) & (slot[None, None, :] < slot[None, :, None]))
    turn = jnp.sum(ahead.astype(jnp.int32), axis=2)
    tile_order = jnp.sum(
        jnp.where(turn[:, None, :] == slot[None, :, None], slot[None, None, :], 0), axis=2
    )
    below = entry[:, :, None] < jnp.arange(LIST_ENTRIES + 1, dtype=jnp.int32)[None, None, :]
    entry_bounds = jnp.einsum(
        "os,lse->loe",
        jnp.ones((8, slot.shape[0]), jnp.bfloat16),
        below.astype(jnp.bfloat16),
        preferred_element_type=jnp.float32,
    )[:, 0].astype(jnp.int32)
    def brought(at):
        since = jnp.where(at < FIRST_PAIR, at, at - FIRST_PAIR)
        return jnp.where((since < ALONE) & (at < LIST_ENTRIES), NOWHERE, at).reshape(-1)

    second_at = jnp.where(at_end == 1, second_at.reshape(-1), brought(second_at))
    first_at = brought(first_at)

    source, tile_order = lax.optimization_barrier((source, tile_order))
    chosen = sent_half(1)

    def through_lists(got, chosen, tiles, tile_target, tile_place, density):
        chosen, got = lax.optimization_barrier((chosen, got))
        got = [got, exchanged(chosen)]
        slabs = [passed_along(density, "col", -offset) for offset in range(STEPS)]
        slabs[0] = density
        groups = {
            0: [(1, 0), (0, 1), (0, 3)],
            1: [(0, 2), (0, 4), (1, 1), (1, 2), (1, 3), (1, 4)],
            3: [(0, 6), (0, 7), (0, 8), (0, 9), (1, 5), (1, 6)],
            5: [(0, 10), (0, 11), (0, 12), (1, 7), (1, 8), (1, 9)],
            7: [(1, 10), (1, 11), (1, 12)],
        }

        def sums_of(group, after):
            parts = 1 if max(chunk for _, chunk in group) * CHUNK < FIRST_PAIR else 2
            return listed_sums(got[:parts], tile_order, entry_bounds, group, after)

        chunks = chain_sums(sums_of, groups, slabs)
        place = jnp.stack([me, at_end]).astype(jnp.int32)
        return contracted(place, first_at, second_at, slabs, chunks)

    def round_the_ring(got, chosen, *args):
        return on_device_ring(*args)

    return lax.cond(
        fits,
        through_lists,
        round_the_ring,
        got[0],
        chosen,
        tiles,
        tile_target,
        tile_place,
        density,
    )


def solution(mesh):
    in_specs = (
        P(("row", "col"), None, None),
        P(("row", "col"), None),
        P(("row", "col")),
        P("col", "row"),
    )
    out_specs = P("col", "row")
    on_device = on_device_chain if mesh.shape["row"] == STEPS else on_device_ring
    return jax.shard_map(
        on_device, mesh=mesh, in_specs=in_specs, out_specs=out_specs, check_vma=False
    )
```

```python
import functools

import jax
import jax.numpy as jnp
from jax import lax
from jax.experimental import pallas as pl
from jax.experimental.pallas import tpu as pltpu
from jax.sharding import PartitionSpec as P

ROW_BLOCKS_DEV = 24
K_BLOCKS = 4
STEPS = 4
POSITIONS = 96

INWARD = [(0, 1), (3, 2)]
ACROSS = [(1, 2), (2, 1)]
OUTWARD = [(1, 0), (2, 3)]
LAG = 2

CHUNK = 24
ALONE, ONE_BEFORE, FIRST_PAIR, LAST_PAIR = 24, 72, 120, 192
LIST_ENTRIES = FIRST_PAIR + LAST_PAIR
FIRST_DONE = 240
NOWHERE = 1 << 15
ROW_TILE = 4
SUM_VMEM_BYTES = 24 * 1024 * 1024
CONTRACT_VMEM_BYTES = 56 * 1024 * 1024
SMALL = pl.CostEstimate(flops=1000, bytes_accessed=1000, transcendentals=0)


def passed_along(value, axis, steps):
    count = lax.axis_size(axis)
    pairs = [(source, (source + steps) % count) for source in range(count)]
    return lax.ppermute(value, axis, pairs)


def tile_capacity(tile_count, devices):
    return max(2, (2 * tile_count + devices - 1) // devices)


def ranks_of(targets):
    order = jnp.arange(targets.shape[0], dtype=jnp.int32)
    same_target = targets[:, None] == targets[None, :]
    earlier = order[None, :] < order[:, None]
    return jnp.sum((same_target & earlier).astype(jnp.int32), axis=1)


def on_device_ring(tiles, tile_target, tile_place, density):
    row_count = lax.axis_size("row")
    col_count = lax.axis_size("col")
    devices = row_count * col_count
    tile_count = tiles.shape[0]
    tile_size = tiles.shape[1]
    capacity = tile_capacity(tile_count, devices)
    slots = devices * capacity
    targets = tile_target[:, 0]
    order = jnp.arange(tile_count, dtype=jnp.int32)
    slot_of = targets * capacity + ranks_of(targets)
    hits = slot_of[None, :] == jnp.arange(slots, dtype=jnp.int32)[:, None]
    filled = jnp.any(hits, axis=1)
    source = jnp.sum(jnp.where(hits, order[None, :], 0), axis=1)
    send_tiles = jnp.take(tiles, source, axis=0)
    send_places = jnp.where(filled, jnp.take(tile_place, source), -1)
    got_tiles, got_places = (
        lax.all_to_all(send_tiles, ("row", "col"), split_axis=0, concat_axis=0, tiled=True),
        lax.all_to_all(send_places, ("row", "col"), split_axis=0, concat_axis=0, tiled=True),
    )
    got_tiles = got_tiles.reshape(slots, tile_size * tile_size)
    selector = (got_places[None, :] == jnp.arange(POSITIONS, dtype=jnp.int32)[:, None]).astype(
        jnp.bfloat16
    )
    dense = jnp.dot(selector, got_tiles, preferred_element_type=jnp.float32)
    dense = dense.reshape(ROW_BLOCKS_DEV, K_BLOCKS, tile_size, tile_size).transpose(0, 2, 1, 3)
    panel = dense.reshape(ROW_BLOCKS_DEV * tile_size, K_BLOCKS * tile_size).astype(jnp.bfloat16)
    total = jnp.zeros((panel.shape[0], density.shape[1]), jnp.float32)
    left, right = (panel, density)
    for offset in range(STEPS):
        total = total + jnp.dot(left, right, preferred_element_type=jnp.float32)
        if offset + 1 < STEPS:
            left = passed_along(left, "row", -1)
            right = passed_along(right, "col", -1)
    return total.astype(jnp.bfloat16)


def picked(tiles, source):
    count = source.shape[0]

    def kernel(source_ref, tiles_ref, out_ref):
        def one(slot, carry):
            out_ref[slot] = tiles_ref[source_ref[slot]]
            return carry

        lax.fori_loop(0, count, one, 0, unroll=4)

    return pl.pallas_call(
        kernel,
        out_shape=jax.ShapeDtypeStruct((count,) + tiles.shape[1:], tiles.dtype),
        grid_spec=pltpu.PrefetchScalarGridSpec(
            num_scalar_prefetch=1,
            grid=(),
            in_specs=[pl.BlockSpec(memory_space=pltpu.VMEM)],
            out_specs=pl.BlockSpec(memory_space=pltpu.VMEM),
        ),
        compiler_params=pltpu.CompilerParams(vmem_limit_bytes=SUM_VMEM_BYTES),
        cost_estimate=SMALL,
        name="pick_tiles",
    )(source, tiles)


def hops_before(chunk):
    at = chunk * CHUNK
    at = at if at < FIRST_PAIR else at - FIRST_PAIR
    return 0 if at < ALONE else 1 if at < ONE_BEFORE else 2


def listed_sums(got, order, bounds, wanted, after):
    tile = got[0].shape[1:]
    slots = got[0].shape[0]
    parts = len(got)
    count = len(wanted)

    def kernel(order_ref, bounds_ref, *refs):
        got_refs, out_refs = refs[:parts], refs[-2 - count : -2]
        held, sems = refs[-2:]
        copies = [
            pltpu.make_async_copy(got_ref, held.at[pl.ds(part * slots, slots)], sems.at[part])
            for part, got_ref in enumerate(got_refs)
        ]
        for copy in copies:
            copy.start()
        for copy in copies:
            copy.wait()
        for (which, chunk), out in zip(wanted, out_refs):

            def total(entry, carry, which=which, chunk=chunk, out=out):
                def add(at, value):
                    return value + held[order_ref[which, at]].astype(jnp.float32)

                at = chunk * CHUNK + entry
                value = lax.fori_loop(
                    bounds_ref[which, at],
                    bounds_ref[which, at + 1],
                    add,
                    jnp.zeros(tile, jnp.float32),
                )
                out[entry] = value.astype(out.dtype)
                return carry

            lax.fori_loop(0, CHUNK, total, 0)

    out = pl.pallas_call(
        kernel,
        out_shape=[jax.ShapeDtypeStruct((CHUNK,) + tile, got[0].dtype)] * count,
        grid_spec=pltpu.PrefetchScalarGridSpec(
            num_scalar_prefetch=2,
            grid=(),
            in_specs=[pl.BlockSpec(memory_space=pl.ANY)] * (parts + len(after)),
            out_specs=[pl.BlockSpec(memory_space=pltpu.VMEM)] * count,
            scratch_shapes=[
                pltpu.VMEM((parts * slots,) + tile, got[0].dtype),
                pltpu.SemaphoreType.DMA((parts,)),
            ],
        ),
        compiler_params=pltpu.CompilerParams(vmem_limit_bytes=SUM_VMEM_BYTES),
        cost_estimate=SMALL,
        name="sum_tiles",
    )(order, bounds, *got, *after)
    return dict(zip(wanted, out))


def added(one, other, after):
    def kernel(one_ref, other_ref, *refs):
        out_ref = refs[-1]

        def add(entry, carry):
            out_ref[entry] = one_ref[entry] + other_ref[entry]
            return carry

        lax.fori_loop(0, one.shape[0], add, 0, unroll=4)

    held = pl.BlockSpec(memory_space=pltpu.VMEM)
    return pl.pallas_call(
        kernel,
        out_shape=jax.ShapeDtypeStruct(one.shape, one.dtype),
        in_specs=[held, held] + [pl.BlockSpec(memory_space=pl.ANY)] * len(after),
        out_specs=held,
        compiler_params=pltpu.CompilerParams(vmem_limit_bytes=SUM_VMEM_BYTES),
        cost_estimate=SMALL,
        name="add_tiles",
    )(one, other, *after)


def chain_sums(sums_of, groups, slabs):
    count = LIST_ENTRIES // CHUNK
    pair_at = FIRST_PAIR // CHUNK
    near, inward, across, outward = {}, {}, {}, {}
    listed = {}
    last = None

    def sums(group):
        nonlocal last
        listed.update(sums_of(group, [] if last is None else [last]))
        last = listed[group[0]]

    def summed(one, other, after):
        nonlocal last
        last = added(one, other, [last] + after)
        return last

    def enter(chunk):
        if chunk < count and hops_before(chunk) == 2:
            inward[chunk] = lax.ppermute(listed[0, chunk], "row", INWARD)

    def cross(chunk):
        if chunk < count and hops_before(chunk):
            near[chunk] = listed[0, chunk]
            if hops_before(chunk) == 2:
                near[chunk] = summed(near[chunk], inward[chunk], [])
            across[chunk] = lax.ppermute(near[chunk], "row", ACROSS)

    def leave(chunk):
        moving = listed[1, chunk]
        if hops_before(chunk):
            after = [outward[chunk - LAG]] if chunk >= LAG else []
            if chunk > pair_at and (chunk - pair_at) % 2 == 0:
                after += slabs[(chunk - pair_at) // 2 :][:1]
            moving = summed(moving, across[chunk], after)
        outward[chunk] = lax.ppermute(moving, "row", OUTWARD)

    sums(groups[0])
    leave(0)
    cross(1)
    enter(3)
    sums(groups[1])
    cross(2)
    enter(4)
    for chunk in range(1, count):
        leave(chunk)
        cross(chunk + LAG)
        if chunk > 1 and chunk in groups:
            sums(groups[chunk])
        enter(chunk + 2 * LAG)
    return near, across, outward


def contracted(place, first_at, second_at, slabs, chunks, rows, span, before, out_dtype):
    low, high = span
    near, across, outward = (
        {at - low: part[at] for at in range(low, high) if at in part} for part in chunks
    )
    count = high - low
    entries = count * CHUNK
    tile = outward[0].shape[1]
    depth = K_BLOCKS * tile
    columns = slabs[0].shape[1]
    row_count = len(slabs)
    panels = len(rows)
    steps = ROW_BLOCKS_DEV // ROW_TILE
    col_tile = min(512, columns)
    both = sorted(near)

    def kernel(place_ref, first_ref, second_ref, *refs):
        near_refs = dict(zip(both, refs))
        across_refs = dict(zip(both, refs[len(both) :]))
        outward_refs = refs[2 * len(both) : 2 * len(both) + count]
        slab_refs = refs[2 * len(both) + count : 2 * len(both) + count + row_count]
        out_ref, near_held, far_held, slab_held, left, sems = refs[-6:]
        before_ref = refs[-7]
        step = pl.program_id(0)
        me, end = place_ref[0], place_ref[1]

        @pl.when(step == 0)
        def _():
            for part in range(count):
                there = pl.ds(part * CHUNK, CHUNK)

                def from_outward(part=part, there=there):
                    pltpu.make_async_copy(
                        outward_refs[part], far_held.at[there], sems.at[2 * part + 1]
                    ).start()

                if part not in near_refs:
                    from_outward()
                    continue
                pltpu.make_async_copy(
                    near_refs[part], near_held.at[there], sems.at[2 * part]
                ).start()
                pl.when(end == 1)(from_outward)

                @pl.when(end == 0)
                def _(part=part, there=there):
                    pltpu.make_async_copy(
                        across_refs[part], far_held.at[there], sems.at[2 * part + 1]
                    ).start()

            for panel, row in enumerate(rows):
                offset = lax.rem(row - me + row_count, row_count)
                for which in range(row_count):

                    @pl.when(offset == which)
                    def _(panel=panel, which=which):
                        pltpu.make_async_copy(
                            slab_refs[which],
                            slab_held.at[pl.ds(panel * depth, depth)],
                            sems.at[2 * count + panel],
                        ).start()

            near_held[entries] = jnp.zeros((tile, tile), near_held.dtype)
            far_held[entries] = jnp.zeros((tile, tile), far_held.dtype)
            for part in range(count):
                there = pl.ds(part * CHUNK, CHUNK)
                if part in near_refs:
                    pltpu.make_async_copy(
                        near_refs[part], near_held.at[there], sems.at[2 * part]
                    ).wait()
                pltpu.make_async_copy(
                    outward_refs[part], far_held.at[there], sems.at[2 * part + 1]
                ).wait()
            for panel in range(panels):
                pltpu.make_async_copy(
                    slab_refs[0],
                    slab_held.at[pl.ds(panel * depth, depth)],
                    sems.at[2 * count + panel],
                ).wait()

        def fill(row_block, carry):
            for panel, row in enumerate(rows):
                for k in range(K_BLOCKS):
                    at = row * POSITIONS + (step * ROW_TILE + row_block) * K_BLOCKS + k
                    one = jnp.minimum(first_ref[at] - low * CHUNK, entries)
                    other = jnp.minimum(second_ref[at] - low * CHUNK, entries)
                    there = (panel * K_BLOCKS + k) * tile
                    left[
                        pl.ds(pl.multiple_of(row_block * tile, tile), tile),
                        there : there + tile,
                    ] = near_held[one] + far_held[other]
            return carry

        lax.fori_loop(0, ROW_TILE, fill, 0)
        for column in range(0, columns, col_tile):
            part = slice(column, column + col_tile)
            product = jnp.dot(left[...], slab_held[:, part], preferred_element_type=jnp.float32)
            if before is not None:
                product = product + before_ref[:, part]
            out_ref[:, part] = product.astype(out_ref.dtype)

    anywhere = pl.BlockSpec(memory_space=pl.ANY)
    blocked = pl.BlockSpec((ROW_TILE * tile, columns), lambda step, *_: (step, 0))
    operands = (place, first_at, second_at)
    operands += tuple(near[part] for part in both) + tuple(across[part] for part in both)
    operands += tuple(outward[part] for part in range(count)) + tuple(slabs)
    extra = () if before is None else (before,)
    return pl.pallas_call(
        kernel,
        out_shape=jax.ShapeDtypeStruct((ROW_BLOCKS_DEV * tile, columns), out_dtype),
        grid_spec=pltpu.PrefetchScalarGridSpec(
            num_scalar_prefetch=3,
            grid=(steps,),
            in_specs=[anywhere] * (len(operands) - 3) + [blocked] * len(extra),
            out_specs=blocked,
            scratch_shapes=[
                pltpu.VMEM((entries + 1, tile, tile), slabs[0].dtype),
                pltpu.VMEM((entries + 1, tile, tile), slabs[0].dtype),
                pltpu.VMEM((panels * depth, columns), slabs[0].dtype),
                pltpu.VMEM((ROW_TILE * tile, panels * depth), slabs[0].dtype),
                pltpu.SemaphoreType.DMA((2 * count + panels,)),
            ],
        ),
        compiler_params=pltpu.CompilerParams(vmem_limit_bytes=CONTRACT_VMEM_BYTES),
        cost_estimate=SMALL,
        name="contract_panels",
    )(*operands, *extra)


def on_device_chain(tiles, tile_target, tile_place, density):
    row_count = lax.axis_size("row")
    col_count = lax.axis_size("col")
    devices = row_count * col_count
    tile_count, tile_size = tiles.shape[:2]
    capacity = tile_capacity(tile_count, devices)
    plane_slots = col_count * capacity
    me = lax.axis_index("row")
    column = lax.axis_index("col")
    at_end = ((me == 0) | (me == row_count - 1)).astype(jnp.int32)

    targets = tile_target[:, 0]
    codes = jnp.broadcast_to(targets * POSITIONS + tile_place, (devices, tile_count))
    codes = lax.all_to_all(codes, ("row", "col"), split_axis=0, concat_axis=0, tiled=True)
    order = jnp.arange(tile_count, dtype=jnp.int32)
    slot_of = targets * capacity + ranks_of(targets)
    hits = slot_of[None, :] == jnp.arange(devices * capacity, dtype=jnp.int32)[:, None]
    source = jnp.sum(jnp.where(hits, order[None, :], 0), axis=1)

    def exchanged(chosen):
        return lax.all_to_all(chosen, "col", split_axis=0, concat_axis=0, tiled=True)

    half = row_count // 2
    source = source.reshape(2, half, col_count, capacity)
    source = source.transpose(0, 2, 1, 3).reshape(2, half * plane_slots)

    def sent_half(which):
        return picked(tiles, source[which])

    got = [exchanged(sent_half(0))]
    codes = codes.reshape(row_count, col_count * tile_count)
    code_target = codes // POSITIONS
    code_place = codes % POSITIONS
    by_target = (code_target[:, None, :] == jnp.arange(devices, dtype=jnp.int32)[None, :, None])
    by_place = (code_place[:, None, :] == jnp.arange(POSITIONS, dtype=jnp.int32)[None, :, None])
    held = jnp.einsum(
        "ptn,pqn->ptq",
        by_target.astype(jnp.bfloat16),
        by_place.astype(jnp.bfloat16),
        preferred_element_type=jnp.float32,
    )
    filled = held > 0
    classes = jnp.stack(
        [
            jnp.stack([~filled[a] & ~filled[b] & filled[c], ~filled[a] & filled[b], filled[a]])
            for a, b, c in ((0, 1, 2), (3, 2, 1))
        ]
    ).astype(jnp.int32)
    classes = classes.reshape(2, 3, 2, half, col_count, POSITIONS)
    counts = jnp.sum(classes, axis=(3, 5))
    begin = jnp.maximum(counts[:, 0, 0], ALONE)
    last_first = jnp.maximum(begin + counts[:, 1, 0], ONE_BEFORE)
    over = jnp.maximum(last_first + counts[:, 2, 0] - FIRST_PAIR, 0)
    later = jnp.maximum(counts[:, 0, 1], ALONE) + FIRST_PAIR
    last = jnp.maximum(later + counts[:, 1, 1], FIRST_PAIR + ONE_BEFORE)
    fits = (last_first <= FIRST_PAIR) & (last + over + counts[:, 2, 1] <= LIST_ENTRIES)
    fits = jnp.all(fits & (last + over <= FIRST_DONE))
    zero = jnp.zeros_like(begin)
    starts = jnp.stack(
        [zero, begin, last_first, zero + FIRST_PAIR, later, last + over, last], axis=1
    )
    starts = lax.dynamic_index_in_dim(starts, column, 2, keepdims=False)
    mine = lax.dynamic_index_in_dim(classes, column, 4, keepdims=False)
    mine = mine.reshape(2, 3, 2, half * POSITIONS)
    spot = jnp.arange(half * POSITIONS, dtype=jnp.int32)
    before_it = spot[:, None] < spot[None, :]
    rank = jnp.sum(jnp.where(before_it, mine[..., None], 0), axis=3)
    at = rank + starts[:, :6].reshape(2, 2, 3).transpose(0, 2, 1)[..., None]
    moved = at - FIRST_PAIR + starts[:, 6][:, None, None, None]
    first_pair = jnp.arange(2)[None, None, :, None] == 0
    at = jnp.where(first_pair & (at >= FIRST_PAIR), moved, at)
    listed = jnp.min(jnp.where(mine > 0, at, NOWHERE), axis=1)
    listed = listed.reshape(2, row_count, POSITIONS)
    is_low = me < row_count // 2
    first_at = jnp.where(is_low, listed[0], listed[1])
    second_at = jnp.where(is_low, listed[1], listed[0])

    near_codes = lax.dynamic_index_in_dim(codes, me, 0, keepdims=False)
    near_codes = near_codes.reshape(col_count, tile_count)
    near_targets = near_codes // POSITIONS
    near_slots = (near_targets * capacity + jax.vmap(ranks_of)(near_targets))[:, None, :]
    near_places = (near_codes % POSITIONS)[:, None, :]
    wanted = jnp.arange(row_count, dtype=jnp.int32)[:, None] * col_count + column
    wanted = (wanted * capacity + jnp.arange(capacity, dtype=jnp.int32)[None, :]).reshape(1, -1, 1)
    got_place = jnp.sum(jnp.where(near_slots == wanted, near_places + 1, 0), axis=2) - 1
    got_place = got_place.reshape(col_count, row_count, capacity).transpose(1, 0, 2)
    got_place = got_place.reshape(row_count, plane_slots, 1)
    at_place = got_place == jnp.arange(POSITIONS, dtype=jnp.int32)[None, None, :]

    def entries_of(table):
        entry = jnp.sum(jnp.where(at_place, table[:, None, :] + 1, 0), axis=2) - 1
        entry = jnp.where(got_place[..., 0] < 0, NOWHERE, entry)
        entry = entry.reshape(2, half, col_count, capacity)
        return entry.transpose(0, 2, 1, 3).reshape(-1)

    entry = jnp.stack([entries_of(first_at), entries_of(second_at)])
    slot = jnp.arange(row_count * plane_slots, dtype=jnp.int32)
    one, other = entry[:, :, None], entry[:, None, :]
    ahead = (other < one) | ((other == one) & (slot[None, None, :] < slot[None, :, None]))
    turn = jnp.sum(ahead.astype(jnp.int32), axis=2)
    tile_order = jnp.sum(
        jnp.where(turn[:, None, :] == slot[None, :, None], slot[None, None, :], 0), axis=2
    )
    below = entry[:, :, None] < jnp.arange(LIST_ENTRIES + 1, dtype=jnp.int32)[None, None, :]
    entry_bounds = jnp.einsum(
        "os,lse->loe",
        jnp.ones((8, slot.shape[0]), jnp.bfloat16),
        below.astype(jnp.bfloat16),
        preferred_element_type=jnp.float32,
    )[:, 0].astype(jnp.int32)
    def brought(at):
        since = jnp.where(at < FIRST_PAIR, at, at - FIRST_PAIR)
        return jnp.where((since < ALONE) & (at < LIST_ENTRIES), NOWHERE, at).reshape(-1)

    second_at = jnp.where(at_end == 1, second_at.reshape(-1), brought(second_at))
    first_at = brought(first_at)

    source, tile_order = lax.optimization_barrier((source, tile_order))
    chosen = sent_half(1)

    def through_lists(got, chosen, tiles, tile_target, tile_place, density):
        chosen, got = lax.optimization_barrier((chosen, got))
        got = [got, exchanged(chosen)]
        slabs = [passed_along(density, "col", -offset) for offset in range(STEPS)]
        slabs[0] = density
        groups = {
            0: [(1, 0), (0, 1), (0, 3)],
            1: [(0, 2), (0, 4), (1, 1), (1, 2), (1, 3), (1, 4)],
            3: [(0, 6), (0, 7), (0, 8), (0, 9), (1, 5), (1, 6)],
            6: [(0, 10), (0, 11), (0, 12), (1, 7), (1, 8), (1, 9)],
            8: [(1, 10), (1, 11), (1, 12)],
        }

        def sums_of(group, after):
            parts = 1 if max(chunk for _, chunk in group) * CHUNK < FIRST_PAIR else 2
            return listed_sums(got[:parts], tile_order, entry_bounds, group, after)

        chunks = chain_sums(sums_of, groups, slabs)
        place = jnp.stack([me, at_end]).astype(jnp.int32)
        common = (place, first_at, second_at, slabs, chunks)
        early, late = FIRST_DONE // CHUNK, FIRST_PAIR // CHUNK
        total = contracted(*common, range(half), (0, early), None, jnp.float32)
        end = LIST_ENTRIES // CHUNK
        return contracted(*common, range(half, row_count), (late, end), total, density.dtype)

    def round_the_ring(got, chosen, *args):
        return on_device_ring(*args)

    return lax.cond(
        fits,
        through_lists,
        round_the_ring,
        got[0],
        chosen,
        tiles,
        tile_target,
        tile_place,
        density,
    )


def solution(mesh):
    in_specs = (
        P(("row", "col"), None, None),
        P(("row", "col"), None),
        P(("row", "col")),
        P("col", "row"),
    )
    out_specs = P("col", "row")
    on_device = on_device_chain if mesh.shape["row"] == STEPS else on_device_ring
    return jax.shard_map(
        on_device, mesh=mesh, in_specs=in_specs, out_specs=out_specs, check_vma=False
    )
```

```python
import functools

import jax
import jax.numpy as jnp
from jax import lax
from jax.experimental import pallas as pl
from jax.experimental.pallas import tpu as pltpu
from jax.sharding import PartitionSpec as P

ROW_BLOCKS_DEV = 24
K_BLOCKS = 4
STEPS = 4
POSITIONS = 96

INWARD = [(0, 1), (3, 2)]
ACROSS = [(1, 2), (2, 1)]
OUTWARD = [(1, 0), (2, 3)]
LAG = 2

CHUNK = 24
ALONE, ONE_BEFORE, FIRST_PAIR, LAST_PAIR = 24, 72, 120, 192
LIST_ENTRIES = FIRST_PAIR + LAST_PAIR
FIRST_DONE = 264
NOWHERE = 1 << 15
ROW_TILE = 4
SUM_VMEM_BYTES = 24 * 1024 * 1024
CONTRACT_VMEM_BYTES = 56 * 1024 * 1024
SMALL = pl.CostEstimate(flops=1000, bytes_accessed=1000, transcendentals=0)


def passed_along(value, axis, steps):
    count = lax.axis_size(axis)
    pairs = [(source, (source + steps) % count) for source in range(count)]
    return lax.ppermute(value, axis, pairs)


def tile_capacity(tile_count, devices):
    return max(2, (2 * tile_count + devices - 1) // devices)


def ranks_of(targets):
    order = jnp.arange(targets.shape[0], dtype=jnp.int32)
    same_target = targets[:, None] == targets[None, :]
    earlier = order[None, :] < order[:, None]
    return jnp.sum((same_target & earlier).astype(jnp.int32), axis=1)


def on_device_ring(tiles, tile_target, tile_place, density):
    row_count = lax.axis_size("row")
    col_count = lax.axis_size("col")
    devices = row_count * col_count
    tile_count = tiles.shape[0]
    tile_size = tiles.shape[1]
    capacity = tile_capacity(tile_count, devices)
    slots = devices * capacity
    targets = tile_target[:, 0]
    order = jnp.arange(tile_count, dtype=jnp.int32)
    slot_of = targets * capacity + ranks_of(targets)
    hits = slot_of[None, :] == jnp.arange(slots, dtype=jnp.int32)[:, None]
    filled = jnp.any(hits, axis=1)
    source = jnp.sum(jnp.where(hits, order[None, :], 0), axis=1)
    send_tiles = jnp.take(tiles, source, axis=0)
    send_places = jnp.where(filled, jnp.take(tile_place, source), -1)
    got_tiles, got_places = (
        lax.all_to_all(send_tiles, ("row", "col"), split_axis=0, concat_axis=0, tiled=True),
        lax.all_to_all(send_places, ("row", "col"), split_axis=0, concat_axis=0, tiled=True),
    )
    got_tiles = got_tiles.reshape(slots, tile_size * tile_size)
    selector = (got_places[None, :] == jnp.arange(POSITIONS, dtype=jnp.int32)[:, None]).astype(
        jnp.bfloat16
    )
    dense = jnp.dot(selector, got_tiles, preferred_element_type=jnp.float32)
    dense = dense.reshape(ROW_BLOCKS_DEV, K_BLOCKS, tile_size, tile_size).transpose(0, 2, 1, 3)
    panel = dense.reshape(ROW_BLOCKS_DEV * tile_size, K_BLOCKS * tile_size).astype(jnp.bfloat16)
    total = jnp.zeros((panel.shape[0], density.shape[1]), jnp.float32)
    left, right = (panel, density)
    for offset in range(STEPS):
        total = total + jnp.dot(left, right, preferred_element_type=jnp.float32)
        if offset + 1 < STEPS:
            left = passed_along(left, "row", -1)
            right = passed_along(right, "col", -1)
    return total.astype(jnp.bfloat16)


def picked(tiles, source):
    count = source.shape[0]

    def kernel(source_ref, tiles_ref, out_ref):
        def one(slot, carry):
            out_ref[slot] = tiles_ref[source_ref[slot]]
            return carry

        lax.fori_loop(0, count, one, 0, unroll=4)

    return pl.pallas_call(
        kernel,
        out_shape=jax.ShapeDtypeStruct((count,) + tiles.shape[1:], tiles.dtype),
        grid_spec=pltpu.PrefetchScalarGridSpec(
            num_scalar_prefetch=1,
            grid=(),
            in_specs=[pl.BlockSpec(memory_space=pltpu.VMEM)],
            out_specs=pl.BlockSpec(memory_space=pltpu.VMEM),
        ),
        compiler_params=pltpu.CompilerParams(vmem_limit_bytes=SUM_VMEM_BYTES),
        cost_estimate=SMALL,
        name="pick_tiles",
    )(source, tiles)


def hops_before(chunk):
    at = chunk * CHUNK
    at = at if at < FIRST_PAIR else at - FIRST_PAIR
    return 0 if at < ALONE else 1 if at < ONE_BEFORE else 2


def listed_sums(got, order, bounds, wanted, after):
    tile = got[0].shape[1:]
    slots = got[0].shape[0]
    parts = len(got)
    count = len(wanted)

    def kernel(order_ref, bounds_ref, *refs):
        got_refs, out_refs = refs[:parts], refs[-2 - count : -2]
        held, sems = refs[-2:]
        copies = [
            pltpu.make_async_copy(got_ref, held.at[pl.ds(part * slots, slots)], sems.at[part])
            for part, got_ref in enumerate(got_refs)
        ]
        for copy in copies:
            copy.start()
        for copy in copies:
            copy.wait()
        for (which, chunk), out in zip(wanted, out_refs):

            def total(entry, carry, which=which, chunk=chunk, out=out):
                def add(at, value):
                    return value + held[order_ref[which, at]].astype(jnp.float32)

                at = chunk * CHUNK + entry
                value = lax.fori_loop(
                    bounds_ref[which, at],
                    bounds_ref[which, at + 1],
                    add,
                    jnp.zeros(tile, jnp.float32),
                )
                out[entry] = value.astype(out.dtype)
                return carry

            lax.fori_loop(0, CHUNK, total, 0)

    out = pl.pallas_call(
        kernel,
        out_shape=[jax.ShapeDtypeStruct((CHUNK,) + tile, got[0].dtype)] * count,
        grid_spec=pltpu.PrefetchScalarGridSpec(
            num_scalar_prefetch=2,
            grid=(),
            in_specs=[pl.BlockSpec(memory_space=pl.ANY)] * (parts + len(after)),
            out_specs=[pl.BlockSpec(memory_space=pltpu.VMEM)] * count,
            scratch_shapes=[
                pltpu.VMEM((parts * slots,) + tile, got[0].dtype),
                pltpu.SemaphoreType.DMA((parts,)),
            ],
        ),
        compiler_params=pltpu.CompilerParams(vmem_limit_bytes=SUM_VMEM_BYTES),
        cost_estimate=SMALL,
        name="sum_tiles",
    )(order, bounds, *got, *after)
    return dict(zip(wanted, out))


def added(one, other, after):
    def kernel(one_ref, other_ref, *refs):
        out_ref = refs[-1]

        def add(entry, carry):
            out_ref[entry] = one_ref[entry] + other_ref[entry]
            return carry

        lax.fori_loop(0, one.shape[0], add, 0, unroll=4)

    held = pl.BlockSpec(memory_space=pltpu.VMEM)
    return pl.pallas_call(
        kernel,
        out_shape=jax.ShapeDtypeStruct(one.shape, one.dtype),
        in_specs=[held, held] + [pl.BlockSpec(memory_space=pl.ANY)] * len(after),
        out_specs=held,
        compiler_params=pltpu.CompilerParams(vmem_limit_bytes=SUM_VMEM_BYTES),
        cost_estimate=SMALL,
        name="add_tiles",
    )(one, other, *after)


def chain_sums(sums_of, groups, slabs):
    count = LIST_ENTRIES // CHUNK
    pair_at = FIRST_PAIR // CHUNK
    near, inward, across, outward = {}, {}, {}, {}
    listed = {}
    last = None

    def sums(group):
        nonlocal last
        listed.update(sums_of(group, [] if last is None else [last]))
        last = listed[group[0]]

    def summed(one, other, after):
        nonlocal last
        last = added(one, other, [last] + after)
        return last

    def enter(chunk):
        if chunk < count and hops_before(chunk) == 2:
            inward[chunk] = lax.ppermute(listed[0, chunk], "row", INWARD)

    def cross(chunk):
        if chunk < count and hops_before(chunk):
            near[chunk] = listed[0, chunk]
            if hops_before(chunk) == 2:
                near[chunk] = summed(near[chunk], inward[chunk], [])
            across[chunk] = lax.ppermute(near[chunk], "row", ACROSS)

    def leave(chunk):
        moving = listed[1, chunk]
        if hops_before(chunk):
            after = [outward[chunk - LAG]] if chunk >= LAG else []
            if chunk > pair_at and (chunk - pair_at) % 2 == 0:
                after += slabs[(chunk - pair_at) // 2 :][:1]
            moving = summed(moving, across[chunk], after)
        outward[chunk] = lax.ppermute(moving, "row", OUTWARD)

    sums(groups[0])
    leave(0)
    cross(1)
    enter(3)
    sums(groups[1])
    cross(2)
    enter(4)
    for chunk in range(1, count):
        leave(chunk)
        cross(chunk + LAG)
        if chunk > 1 and chunk in groups:
            sums(groups[chunk])
        enter(chunk + 2 * LAG)
    return near, across, outward


def contracted(place, first_at, second_at, slabs, chunks, rows, span, before, out_dtype):
    low, high = span
    near, across, outward = (
        {at - low: part[at] for at in range(low, high) if at in part} for part in chunks
    )
    count = high - low
    entries = count * CHUNK
    tile = outward[0].shape[1]
    depth = K_BLOCKS * tile
    columns = slabs[0].shape[1]
    row_count = len(slabs)
    panels = len(rows)
    steps = ROW_BLOCKS_DEV // ROW_TILE
    col_tile = min(512, columns)
    both = sorted(near)

    def kernel(place_ref, first_ref, second_ref, *refs):
        near_refs = dict(zip(both, refs))
        across_refs = dict(zip(both, refs[len(both) :]))
        outward_refs = refs[2 * len(both) : 2 * len(both) + count]
        slab_refs = refs[2 * len(both) + count : 2 * len(both) + count + row_count]
        out_ref, near_held, far_held, slab_held, left, sems = refs[-6:]
        before_ref = refs[-7]
        step = pl.program_id(0)
        me, end = place_ref[0], place_ref[1]

        @pl.when(step == 0)
        def _():
            for part in range(count):
                there = pl.ds(part * CHUNK, CHUNK)

                def from_outward(part=part, there=there):
                    pltpu.make_async_copy(
                        outward_refs[part], far_held.at[there], sems.at[2 * part + 1]
                    ).start()

                if part not in near_refs:
                    from_outward()
                    continue
                pltpu.make_async_copy(
                    near_refs[part], near_held.at[there], sems.at[2 * part]
                ).start()
                pl.when(end == 1)(from_outward)

                @pl.when(end == 0)
                def _(part=part, there=there):
                    pltpu.make_async_copy(
                        across_refs[part], far_held.at[there], sems.at[2 * part + 1]
                    ).start()

            for panel, row in enumerate(rows):
                offset = lax.rem(row - me + row_count, row_count)
                for which in range(row_count):

                    @pl.when(offset == which)
                    def _(panel=panel, which=which):
                        pltpu.make_async_copy(
                            slab_refs[which],
                            slab_held.at[pl.ds(panel * depth, depth)],
                            sems.at[2 * count + panel],
                        ).start()

            near_held[entries] = jnp.zeros((tile, tile), near_held.dtype)
            far_held[entries] = jnp.zeros((tile, tile), far_held.dtype)
            for part in range(count):
                there = pl.ds(part * CHUNK, CHUNK)
                if part in near_refs:
                    pltpu.make_async_copy(
                        near_refs[part], near_held.at[there], sems.at[2 * part]
                    ).wait()
                pltpu.make_async_copy(
                    outward_refs[part], far_held.at[there], sems.at[2 * part + 1]
                ).wait()
            for panel in range(panels):
                pltpu.make_async_copy(
                    slab_refs[0],
                    slab_held.at[pl.ds(panel * depth, depth)],
                    sems.at[2 * count + panel],
                ).wait()

        def fill(row_block, carry):
            for panel, row in enumerate(rows):
                for k in range(K_BLOCKS):
                    at = row * POSITIONS + (step * ROW_TILE + row_block) * K_BLOCKS + k
                    one = jnp.minimum(first_ref[at] - low * CHUNK, entries)
                    other = jnp.minimum(second_ref[at] - low * CHUNK, entries)
                    there = (panel * K_BLOCKS + k) * tile
                    left[
                        pl.ds(pl.multiple_of(row_block * tile, tile), tile),
                        there : there + tile,
                    ] = near_held[one] + far_held[other]
            return carry

        lax.fori_loop(0, ROW_TILE, fill, 0)
        for column in range(0, columns, col_tile):
            part = slice(column, column + col_tile)
            product = jnp.dot(left[...], slab_held[:, part], preferred_element_type=jnp.float32)
            if before is not None:
                product = product + before_ref[:, part]
            out_ref[:, part] = product.astype(out_ref.dtype)

    anywhere = pl.BlockSpec(memory_space=pl.ANY)
    blocked = pl.BlockSpec((ROW_TILE * tile, columns), lambda step, *_: (step, 0))
    operands = (place, first_at, second_at)
    operands += tuple(near[part] for part in both) + tuple(across[part] for part in both)
    operands += tuple(outward[part] for part in range(count)) + tuple(slabs)
    extra = () if before is None else (before,)
    return pl.pallas_call(
        kernel,
        out_shape=jax.ShapeDtypeStruct((ROW_BLOCKS_DEV * tile, columns), out_dtype),
        grid_spec=pltpu.PrefetchScalarGridSpec(
            num_scalar_prefetch=3,
            grid=(steps,),
            in_specs=[anywhere] * (len(operands) - 3) + [blocked] * len(extra),
            out_specs=blocked,
            scratch_shapes=[
                pltpu.VMEM((entries + 1, tile, tile), slabs[0].dtype),
                pltpu.VMEM((entries + 1, tile, tile), slabs[0].dtype),
                pltpu.VMEM((panels * depth, columns), slabs[0].dtype),
                pltpu.VMEM((ROW_TILE * tile, panels * depth), slabs[0].dtype),
                pltpu.SemaphoreType.DMA((2 * count + panels,)),
            ],
        ),
        compiler_params=pltpu.CompilerParams(vmem_limit_bytes=CONTRACT_VMEM_BYTES),
        cost_estimate=SMALL,
        name="contract_panels",
    )(*operands, *extra)


def on_device_chain(tiles, tile_target, tile_place, density):
    row_count = lax.axis_size("row")
    col_count = lax.axis_size("col")
    devices = row_count * col_count
    tile_count, tile_size = tiles.shape[:2]
    capacity = tile_capacity(tile_count, devices)
    plane_slots = col_count * capacity
    me = lax.axis_index("row")
    column = lax.axis_index("col")
    at_end = ((me == 0) | (me == row_count - 1)).astype(jnp.int32)

    targets = tile_target[:, 0]
    codes = jnp.broadcast_to(targets * POSITIONS + tile_place, (devices, tile_count))
    codes = lax.all_to_all(codes, ("row", "col"), split_axis=0, concat_axis=0, tiled=True)
    order = jnp.arange(tile_count, dtype=jnp.int32)
    slot_of = targets * capacity + ranks_of(targets)
    hits = slot_of[None, :] == jnp.arange(devices * capacity, dtype=jnp.int32)[:, None]
    source = jnp.sum(jnp.where(hits, order[None, :], 0), axis=1)

    def exchanged(chosen):
        return lax.all_to_all(chosen, "col", split_axis=0, concat_axis=0, tiled=True)

    half = row_count // 2
    source = source.reshape(2, half, col_count, capacity)
    source = source.transpose(0, 2, 1, 3).reshape(2, half * plane_slots)

    def sent_half(which):
        return picked(tiles, source[which])

    got = [exchanged(sent_half(0))]
    codes = codes.reshape(row_count, col_count * tile_count)
    code_target = codes // POSITIONS
    code_place = codes % POSITIONS
    by_target = (code_target[:, None, :] == jnp.arange(devices, dtype=jnp.int32)[None, :, None])
    by_place = (code_place[:, None, :] == jnp.arange(POSITIONS, dtype=jnp.int32)[None, :, None])
    held = jnp.einsum(
        "ptn,pqn->ptq",
        by_target.astype(jnp.bfloat16),
        by_place.astype(jnp.bfloat16),
        preferred_element_type=jnp.float32,
    )
    filled = held > 0
    classes = jnp.stack(
        [
            jnp.stack([~filled[a] & ~filled[b] & filled[c], ~filled[a] & filled[b], filled[a]])
            for a, b, c in ((0, 1, 2), (3, 2, 1))
        ]
    ).astype(jnp.int32)
    classes = classes.reshape(2, 3, 2, half, col_count, POSITIONS)
    counts = jnp.sum(classes, axis=(3, 5))
    begin = jnp.maximum(counts[:, 0, 0], ALONE)
    last_first = jnp.maximum(begin + counts[:, 1, 0], ONE_BEFORE)
    over = jnp.maximum(last_first + counts[:, 2, 0] - FIRST_PAIR, 0)
    later = jnp.maximum(counts[:, 0, 1], ALONE) + FIRST_PAIR
    last = jnp.maximum(later + counts[:, 1, 1], FIRST_PAIR + ONE_BEFORE)
    fits = (last_first <= FIRST_PAIR) & (last + over + counts[:, 2, 1] <= LIST_ENTRIES)
    fits = jnp.all(fits & (last + over <= FIRST_DONE))
    zero = jnp.zeros_like(begin)
    starts = jnp.stack(
        [zero, begin, last_first, zero + FIRST_PAIR, later, last + over, last], axis=1
    )
    starts = lax.dynamic_index_in_dim(starts, column, 2, keepdims=False)
    mine = lax.dynamic_index_in_dim(classes, column, 4, keepdims=False)
    mine = mine.reshape(2, 3, 2, half * POSITIONS)
    spot = jnp.arange(half * POSITIONS, dtype=jnp.int32)
    before_it = spot[:, None] < spot[None, :]
    rank = jnp.sum(jnp.where(before_it, mine[..., None], 0), axis=3)
    at = rank + starts[:, :6].reshape(2, 2, 3).transpose(0, 2, 1)[..., None]
    moved = at - FIRST_PAIR + starts[:, 6][:, None, None, None]
    first_pair = jnp.arange(2)[None, None, :, None] == 0
    at = jnp.where(first_pair & (at >= FIRST_PAIR), moved, at)
    listed = jnp.min(jnp.where(mine > 0, at, NOWHERE), axis=1)
    listed = listed.reshape(2, row_count, POSITIONS)
    is_low = me < row_count // 2
    first_at = jnp.where(is_low, listed[0], listed[1])
    second_at = jnp.where(is_low, listed[1], listed[0])

    near_codes = lax.dynamic_index_in_dim(codes, me, 0, keepdims=False)
    near_codes = near_codes.reshape(col_count, tile_count)
    near_targets = near_codes // POSITIONS
    near_slots = (near_targets * capacity + jax.vmap(ranks_of)(near_targets))[:, None, :]
    near_places = (near_codes % POSITIONS)[:, None, :]
    wanted = jnp.arange(row_count, dtype=jnp.int32)[:, None] * col_count + column
    wanted = (wanted * capacity + jnp.arange(capacity, dtype=jnp.int32)[None, :]).reshape(1, -1, 1)
    got_place = jnp.sum(jnp.where(near_slots == wanted, near_places + 1, 0), axis=2) - 1
    got_place = got_place.reshape(col_count, row_count, capacity).transpose(1, 0, 2)
    got_place = got_place.reshape(row_count, plane_slots, 1)
    at_place = got_place == jnp.arange(POSITIONS, dtype=jnp.int32)[None, None, :]

    def entries_of(table):
        entry = jnp.sum(jnp.where(at_place, table[:, None, :] + 1, 0), axis=2) - 1
        entry = jnp.where(got_place[..., 0] < 0, NOWHERE, entry)
        entry = entry.reshape(2, half, col_count, capacity)
        return entry.transpose(0, 2, 1, 3).reshape(-1)

    entry = jnp.stack([entries_of(first_at), entries_of(second_at)])
    slot = jnp.arange(row_count * plane_slots, dtype=jnp.int32)
    one, other = entry[:, :, None], entry[:, None, :]
    ahead = (other < one) | ((other == one) & (slot[None, None, :] < slot[None, :, None]))
    turn = jnp.sum(ahead.astype(jnp.int32), axis=2)
    tile_order = jnp.sum(
        jnp.where(turn[:, None, :] == slot[None, :, None], slot[None, None, :], 0), axis=2
    )
    below = entry[:, :, None] < jnp.arange(LIST_ENTRIES + 1, dtype=jnp.int32)[None, None, :]
    entry_bounds = jnp.einsum(
        "os,lse->loe",
        jnp.ones((8, slot.shape[0]), jnp.bfloat16),
        below.astype(jnp.bfloat16),
        preferred_element_type=jnp.float32,
    )[:, 0].astype(jnp.int32)
    def brought(at):
        since = jnp.where(at < FIRST_PAIR, at, at - FIRST_PAIR)
        return jnp.where((since < ALONE) & (at < LIST_ENTRIES), NOWHERE, at).reshape(-1)

    second_at = jnp.where(at_end == 1, second_at.reshape(-1), brought(second_at))
    first_at = brought(first_at)

    source, tile_order = lax.optimization_barrier((source, tile_order))
    chosen = sent_half(1)

    def through_lists(got, chosen, tiles, tile_target, tile_place, density):
        chosen, got = lax.optimization_barrier((chosen, got))
        got = [got, exchanged(chosen)]
        slabs = [passed_along(density, "col", -offset) for offset in range(STEPS)]
        slabs[0] = density
        groups = {
            0: [(1, 0), (0, 1), (0, 3)],
            1: [(0, 2), (0, 4), (1, 1), (1, 2), (1, 3), (1, 4)],
            3: [(0, 6), (0, 7), (0, 8), (0, 9), (1, 5), (1, 6)],
            6: [(0, 10), (0, 11), (0, 12), (1, 7), (1, 8), (1, 9)],
            8: [(1, 10), (1, 11), (1, 12)],
        }

        def sums_of(group, after):
            parts = 1 if max(chunk for _, chunk in group) * CHUNK < FIRST_PAIR else 2
            return listed_sums(got[:parts], tile_order, entry_bounds, group, after)

        chunks = chain_sums(sums_of, groups, slabs)
        place = jnp.stack([me, at_end]).astype(jnp.int32)
        common = (place, first_at, second_at, slabs, chunks)
        early, late = FIRST_DONE // CHUNK, FIRST_PAIR // CHUNK
        total = contracted(*common, range(half), (0, early), None, jnp.float32)
        end = LIST_ENTRIES // CHUNK
        return contracted(*common, range(half, row_count), (late, end), total, density.dtype)

    def round_the_ring(got, chosen, *args):
        return on_device_ring(*args)

    return lax.cond(
        fits,
        through_lists,
        round_the_ring,
        got[0],
        chosen,
        tiles,
        tile_target,
        tile_place,
        density,
    )


def solution(mesh):
    in_specs = (
        P(("row", "col"), None, None),
        P(("row", "col"), None),
        P(("row", "col")),
        P("col", "row"),
    )
    out_specs = P("col", "row")
    on_device = on_device_chain if mesh.shape["row"] == STEPS else on_device_ring
    return jax.shard_map(
        on_device, mesh=mesh, in_specs=in_specs, out_specs=out_specs, check_vma=False
    )
```

```python
import functools

import jax
import jax.numpy as jnp
from jax import lax
from jax.experimental import pallas as pl
from jax.experimental.pallas import tpu as pltpu
from jax.sharding import PartitionSpec as P

ROW_BLOCKS_DEV = 24
K_BLOCKS = 4
STEPS = 4
POSITIONS = 96

INWARD = [(0, 1), (3, 2)]
ACROSS = [(1, 2), (2, 1)]
OUTWARD = [(1, 0), (2, 3)]
LAG = 2

CHUNK = 24
ALONE, ONE_BEFORE, FIRST_PAIR, LAST_PAIR = 24, 72, 120, 192
LIST_ENTRIES = FIRST_PAIR + LAST_PAIR
FIRST_DONE = 264
NOWHERE = 1 << 15
ROW_TILE = 4
SUM_VMEM_BYTES = 18 * 1024 * 1024
CONTRACT_VMEM_BYTES = 56 * 1024 * 1024
SMALL = pl.CostEstimate(flops=1000, bytes_accessed=1000, transcendentals=0)


def passed_along(value, axis, steps):
    count = lax.axis_size(axis)
    pairs = [(source, (source + steps) % count) for source in range(count)]
    return lax.ppermute(value, axis, pairs)


def tile_capacity(tile_count, devices):
    return max(2, (2 * tile_count + devices - 1) // devices)


def ranks_of(targets):
    order = jnp.arange(targets.shape[0], dtype=jnp.int32)
    same_target = targets[:, None] == targets[None, :]
    earlier = order[None, :] < order[:, None]
    return jnp.sum((same_target & earlier).astype(jnp.int32), axis=1)


def on_device_ring(tiles, tile_target, tile_place, density):
    row_count = lax.axis_size("row")
    col_count = lax.axis_size("col")
    devices = row_count * col_count
    tile_count = tiles.shape[0]
    tile_size = tiles.shape[1]
    capacity = tile_capacity(tile_count, devices)
    slots = devices * capacity
    targets = tile_target[:, 0]
    order = jnp.arange(tile_count, dtype=jnp.int32)
    slot_of = targets * capacity + ranks_of(targets)
    hits = slot_of[None, :] == jnp.arange(slots, dtype=jnp.int32)[:, None]
    filled = jnp.any(hits, axis=1)
    source = jnp.sum(jnp.where(hits, order[None, :], 0), axis=1)
    send_tiles = jnp.take(tiles, source, axis=0)
    send_places = jnp.where(filled, jnp.take(tile_place, source), -1)
    got_tiles, got_places = (
        lax.all_to_all(send_tiles, ("row", "col"), split_axis=0, concat_axis=0, tiled=True),
        lax.all_to_all(send_places, ("row", "col"), split_axis=0, concat_axis=0, tiled=True),
    )
    got_tiles = got_tiles.reshape(slots, tile_size * tile_size)
    selector = (got_places[None, :] == jnp.arange(POSITIONS, dtype=jnp.int32)[:, None]).astype(
        jnp.bfloat16
    )
    dense = jnp.dot(selector, got_tiles, preferred_element_type=jnp.float32)
    dense = dense.reshape(ROW_BLOCKS_DEV, K_BLOCKS, tile_size, tile_size).transpose(0, 2, 1, 3)
    panel = dense.reshape(ROW_BLOCKS_DEV * tile_size, K_BLOCKS * tile_size).astype(jnp.bfloat16)
    total = jnp.zeros((panel.shape[0], density.shape[1]), jnp.float32)
    left, right = (panel, density)
    for offset in range(STEPS):
        total = total + jnp.dot(left, right, preferred_element_type=jnp.float32)
        if offset + 1 < STEPS:
            left = passed_along(left, "row", -1)
            right = passed_along(right, "col", -1)
    return total.astype(jnp.bfloat16)


def picked(tiles, source):
    count = source.shape[0]

    def kernel(source_ref, tiles_ref, out_ref):
        def one(slot, carry):
            out_ref[slot] = tiles_ref[source_ref[slot]]
            return carry

        lax.fori_loop(0, count, one, 0, unroll=4)

    return pl.pallas_call(
        kernel,
        out_shape=jax.ShapeDtypeStruct((count,) + tiles.shape[1:], tiles.dtype),
        grid_spec=pltpu.PrefetchScalarGridSpec(
            num_scalar_prefetch=1,
            grid=(),
            in_specs=[pl.BlockSpec(memory_space=pltpu.VMEM)],
            out_specs=pl.BlockSpec(memory_space=pltpu.VMEM),
        ),
        compiler_params=pltpu.CompilerParams(vmem_limit_bytes=SUM_VMEM_BYTES),
        cost_estimate=SMALL,
        name="pick_tiles",
    )(source, tiles)


def hops_before(chunk):
    at = chunk * CHUNK
    at = at if at < FIRST_PAIR else at - FIRST_PAIR
    return 0 if at < ALONE else 1 if at < ONE_BEFORE else 2


def listed_sums(got, order, bounds, wanted, after):
    tile = got[0].shape[1:]
    slots = got[0].shape[0]
    parts = len(got)
    count = len(wanted)

    def kernel(order_ref, bounds_ref, *refs):
        got_refs, out_refs = refs[:parts], refs[-2 - count : -2]
        held, sems = refs[-2:]
        copies = [
            pltpu.make_async_copy(got_ref, held.at[pl.ds(part * slots, slots)], sems.at[part])
            for part, got_ref in enumerate(got_refs)
        ]
        for copy in copies:
            copy.start()
        for copy in copies:
            copy.wait()
        for (which, chunk), out in zip(wanted, out_refs):

            def total(entry, carry, which=which, chunk=chunk, out=out):
                def add(at, value):
                    return value + held[order_ref[which, at]].astype(jnp.float32)

                at = chunk * CHUNK + entry
                value = lax.fori_loop(
                    bounds_ref[which, at],
                    bounds_ref[which, at + 1],
                    add,
                    jnp.zeros(tile, jnp.float32),
                )
                out[entry] = value.astype(out.dtype)
                return carry

            lax.fori_loop(0, CHUNK, total, 0)

    out = pl.pallas_call(
        kernel,
        out_shape=[jax.ShapeDtypeStruct((CHUNK,) + tile, got[0].dtype)] * count,
        grid_spec=pltpu.PrefetchScalarGridSpec(
            num_scalar_prefetch=2,
            grid=(),
            in_specs=[pl.BlockSpec(memory_space=pl.ANY)] * (parts + len(after)),
            out_specs=[pl.BlockSpec(memory_space=pltpu.VMEM)] * count,
            scratch_shapes=[
                pltpu.VMEM((parts * slots,) + tile, got[0].dtype),
                pltpu.SemaphoreType.DMA((parts,)),
            ],
        ),
        compiler_params=pltpu.CompilerParams(vmem_limit_bytes=SUM_VMEM_BYTES),
        cost_estimate=SMALL,
        name="sum_tiles",
    )(order, bounds, *got, *after)
    return dict(zip(wanted, out))


def added(one, other, after):
    def kernel(one_ref, other_ref, *refs):
        out_ref = refs[-1]

        def add(entry, carry):
            out_ref[entry] = one_ref[entry] + other_ref[entry]
            return carry

        lax.fori_loop(0, one.shape[0], add, 0, unroll=4)

    held = pl.BlockSpec(memory_space=pltpu.VMEM)
    return pl.pallas_call(
        kernel,
        out_shape=jax.ShapeDtypeStruct(one.shape, one.dtype),
        in_specs=[held, held] + [pl.BlockSpec(memory_space=pl.ANY)] * len(after),
        out_specs=held,
        compiler_params=pltpu.CompilerParams(vmem_limit_bytes=SUM_VMEM_BYTES),
        cost_estimate=SMALL,
        name="add_tiles",
    )(one, other, *after)


def chain_sums(sums_of, groups, slabs):
    count = LIST_ENTRIES // CHUNK
    pair_at = FIRST_PAIR // CHUNK
    near, inward, across, outward = {}, {}, {}, {}
    listed = {}
    last = None

    def sums(group):
        nonlocal last
        listed.update(sums_of(group, [] if last is None else [last]))
        last = listed[group[0]]

    def summed(one, other, after):
        nonlocal last
        last = added(one, other, [last] + after)
        return last

    def enter(chunk):
        if chunk < count and hops_before(chunk) == 2:
            inward[chunk] = lax.ppermute(listed[0, chunk], "row", INWARD)

    def cross(chunk):
        if chunk < count and hops_before(chunk):
            near[chunk] = listed[0, chunk]
            if hops_before(chunk) == 2:
                near[chunk] = summed(near[chunk], inward[chunk], [])
            across[chunk] = lax.ppermute(near[chunk], "row", ACROSS)

    def leave(chunk):
        moving = listed[1, chunk]
        if hops_before(chunk):
            after = [outward[chunk - LAG]] if chunk >= LAG else []
            if chunk > pair_at and (chunk - pair_at) % 2 == 0:
                after += slabs[(chunk - pair_at) // 2 :][:1]
            moving = summed(moving, across[chunk], after)
        outward[chunk] = lax.ppermute(moving, "row", OUTWARD)

    sums(groups[0])
    leave(0)
    cross(1)
    enter(3)
    sums(groups[1])
    cross(2)
    enter(4)
    for chunk in range(1, count):
        leave(chunk)
        cross(chunk + LAG)
        if chunk > 1 and chunk in groups:
            sums(groups[chunk])
        enter(chunk + 2 * LAG)
    return near, across, outward


def contracted(place, first_at, second_at, slabs, chunks, rows, span, before, out_dtype):
    low, high = span
    near, across, outward = (
        {at - low: part[at] for at in range(low, high) if at in part} for part in chunks
    )
    count = high - low
    entries = count * CHUNK
    tile = outward[0].shape[1]
    depth = K_BLOCKS * tile
    columns = slabs[0].shape[1]
    row_count = len(slabs)
    panels = len(rows)
    steps = ROW_BLOCKS_DEV // ROW_TILE
    col_tile = min(1024, columns)
    both = sorted(near)

    def kernel(place_ref, first_ref, second_ref, *refs):
        near_refs = dict(zip(both, refs))
        across_refs = dict(zip(both, refs[len(both) :]))
        outward_refs = refs[2 * len(both) : 2 * len(both) + count]
        slab_refs = refs[2 * len(both) + count : 2 * len(both) + count + row_count]
        out_ref, near_held, far_held, slab_held, left, sems = refs[-6:]
        before_ref = refs[-7]
        step = pl.program_id(0)
        me, end = place_ref[0], place_ref[1]

        @pl.when(step == 0)
        def _():
            for part in range(count):
                there = pl.ds(part * CHUNK, CHUNK)

                def from_outward(part=part, there=there):
                    pltpu.make_async_copy(
                        outward_refs[part], far_held.at[there], sems.at[2 * part + 1]
                    ).start()

                if part not in near_refs:
                    from_outward()
                    continue
                pltpu.make_async_copy(
                    near_refs[part], near_held.at[there], sems.at[2 * part]
                ).start()
                pl.when(end == 1)(from_outward)

                @pl.when(end == 0)
                def _(part=part, there=there):
                    pltpu.make_async_copy(
                        across_refs[part], far_held.at[there], sems.at[2 * part + 1]
                    ).start()

            for panel, row in enumerate(rows):
                offset = lax.rem(row - me + row_count, row_count)
                for which in range(row_count):

                    @pl.when(offset == which)
                    def _(panel=panel, which=which):
                        pltpu.make_async_copy(
                            slab_refs[which],
                            slab_held.at[pl.ds(panel * depth, depth)],
                            sems.at[2 * count + panel],
                        ).start()

            near_held[entries] = jnp.zeros((tile, tile), near_held.dtype)
            far_held[entries] = jnp.zeros((tile, tile), far_held.dtype)
            for part in range(count):
                there = pl.ds(part * CHUNK, CHUNK)
                if part in near_refs:
                    pltpu.make_async_copy(
                        near_refs[part], near_held.at[there], sems.at[2 * part]
                    ).wait()
                pltpu.make_async_copy(
                    outward_refs[part], far_held.at[there], sems.at[2 * part + 1]
                ).wait()
            for panel in range(panels):
                pltpu.make_async_copy(
                    slab_refs[0],
                    slab_held.at[pl.ds(panel * depth, depth)],
                    sems.at[2 * count + panel],
                ).wait()

        def fill(row_block, carry):
            for panel, row in enumerate(rows):
                for k in range(K_BLOCKS):
                    at = row * POSITIONS + (step * ROW_TILE + row_block) * K_BLOCKS + k
                    one = jnp.minimum(first_ref[at] - low * CHUNK, entries)
                    other = jnp.minimum(second_ref[at] - low * CHUNK, entries)
                    there = (panel * K_BLOCKS + k) * tile
                    left[
                        pl.ds(pl.multiple_of(row_block * tile, tile), tile),
                        there : there + tile,
                    ] = near_held[one] + far_held[other]
            return carry

        lax.fori_loop(0, ROW_TILE, fill, 0)
        for column in range(0, columns, col_tile):
            part = slice(column, column + col_tile)
            product = jnp.dot(left[...], slab_held[:, part], preferred_element_type=jnp.float32)
            if before is not None:
                product = product + before_ref[:, part]
            out_ref[:, part] = product.astype(out_ref.dtype)

    anywhere = pl.BlockSpec(memory_space=pl.ANY)
    blocked = pl.BlockSpec((ROW_TILE * tile, columns), lambda step, *_: (step, 0))
    operands = (place, first_at, second_at)
    operands += tuple(near[part] for part in both) + tuple(across[part] for part in both)
    operands += tuple(outward[part] for part in range(count)) + tuple(slabs)
    extra = () if before is None else (before,)
    return pl.pallas_call(
        kernel,
        out_shape=jax.ShapeDtypeStruct((ROW_BLOCKS_DEV * tile, columns), out_dtype),
        grid_spec=pltpu.PrefetchScalarGridSpec(
            num_scalar_prefetch=3,
            grid=(steps,),
            in_specs=[anywhere] * (len(operands) - 3) + [blocked] * len(extra),
            out_specs=blocked,
            scratch_shapes=[
                pltpu.VMEM((entries + 1, tile, tile), slabs[0].dtype),
                pltpu.VMEM((entries + 1, tile, tile), slabs[0].dtype),
                pltpu.VMEM((panels * depth, columns), slabs[0].dtype),
                pltpu.VMEM((ROW_TILE * tile, panels * depth), slabs[0].dtype),
                pltpu.SemaphoreType.DMA((2 * count + panels,)),
            ],
        ),
        compiler_params=pltpu.CompilerParams(vmem_limit_bytes=CONTRACT_VMEM_BYTES),
        cost_estimate=SMALL,
        name="contract_panels",
    )(*operands, *extra)


def on_device_chain(tiles, tile_target, tile_place, density):
    row_count = lax.axis_size("row")
    col_count = lax.axis_size("col")
    devices = row_count * col_count
    tile_count, tile_size = tiles.shape[:2]
    capacity = tile_capacity(tile_count, devices)
    plane_slots = col_count * capacity
    me = lax.axis_index("row")
    column = lax.axis_index("col")
    at_end = ((me == 0) | (me == row_count - 1)).astype(jnp.int32)

    targets = tile_target[:, 0]
    codes = jnp.broadcast_to(targets * POSITIONS + tile_place, (devices, tile_count))
    codes = lax.all_to_all(codes, ("row", "col"), split_axis=0, concat_axis=0, tiled=True)
    order = jnp.arange(tile_count, dtype=jnp.int32)
    slot_of = targets * capacity + ranks_of(targets)
    hits = slot_of[None, :] == jnp.arange(devices * capacity, dtype=jnp.int32)[:, None]
    source = jnp.sum(jnp.where(hits, order[None, :], 0), axis=1)

    def exchanged(chosen):
        return lax.all_to_all(chosen, "col", split_axis=0, concat_axis=0, tiled=True)

    half = row_count // 2
    source = source.reshape(2, half, col_count, capacity)
    source = source.transpose(0, 2, 1, 3).reshape(2, half * plane_slots)

    def sent_half(which):
        return picked(tiles, source[which])

    got = [exchanged(sent_half(0))]
    codes = codes.reshape(row_count, col_count * tile_count)
    code_target = codes // POSITIONS
    code_place = codes % POSITIONS
    by_target = (code_target[:, None, :] == jnp.arange(devices, dtype=jnp.int32)[None, :, None])
    by_place = (code_place[:, None, :] == jnp.arange(POSITIONS, dtype=jnp.int32)[None, :, None])
    held = jnp.einsum(
        "ptn,pqn->ptq",
        by_target.astype(jnp.bfloat16),
        by_place.astype(jnp.bfloat16),
        preferred_element_type=jnp.float32,
    )
    filled = held > 0
    classes = jnp.stack(
        [
            jnp.stack([~filled[a] & ~filled[b] & filled[c], ~filled[a] & filled[b], filled[a]])
            for a, b, c in ((0, 1, 2), (3, 2, 1))
        ]
    ).astype(jnp.int32)
    classes = classes.reshape(2, 3, 2, half, col_count, POSITIONS)
    counts = jnp.sum(classes, axis=(3, 5))
    begin = jnp.maximum(counts[:, 0, 0], ALONE)
    last_first = jnp.maximum(begin + counts[:, 1, 0], ONE_BEFORE)
    over = jnp.maximum(last_first + counts[:, 2, 0] - FIRST_PAIR, 0)
    later = jnp.maximum(counts[:, 0, 1], ALONE) + FIRST_PAIR
    last = jnp.maximum(later + counts[:, 1, 1], FIRST_PAIR + ONE_BEFORE)
    fits = (last_first <= FIRST_PAIR) & (last + over + counts[:, 2, 1] <= LIST_ENTRIES)
    fits = jnp.all(fits & (last + over <= FIRST_DONE))
    zero = jnp.zeros_like(begin)
    starts = jnp.stack(
        [zero, begin, last_first, zero + FIRST_PAIR, later, last + over, last], axis=1
    )
    starts = lax.dynamic_index_in_dim(starts, column, 2, keepdims=False)
    mine = lax.dynamic_index_in_dim(classes, column, 4, keepdims=False)
    mine = mine.reshape(2, 3, 2, half * POSITIONS)
    spot = jnp.arange(half * POSITIONS, dtype=jnp.int32)
    before_it = spot[:, None] < spot[None, :]
    rank = jnp.sum(jnp.where(before_it, mine[..., None], 0), axis=3)
    at = rank + starts[:, :6].reshape(2, 2, 3).transpose(0, 2, 1)[..., None]
    moved = at - FIRST_PAIR + starts[:, 6][:, None, None, None]
    first_pair = jnp.arange(2)[None, None, :, None] == 0
    at = jnp.where(first_pair & (at >= FIRST_PAIR), moved, at)
    listed = jnp.min(jnp.where(mine > 0, at, NOWHERE), axis=1)
    listed = listed.reshape(2, row_count, POSITIONS)
    is_low = me < row_count // 2
    first_at = jnp.where(is_low, listed[0], listed[1])
    second_at = jnp.where(is_low, listed[1], listed[0])

    near_codes = lax.dynamic_index_in_dim(codes, me, 0, keepdims=False)
    near_codes = near_codes.reshape(col_count, tile_count)
    near_targets = near_codes // POSITIONS
    near_slots = (near_targets * capacity + jax.vmap(ranks_of)(near_targets))[:, None, :]
    near_places = (near_codes % POSITIONS)[:, None, :]
    wanted = jnp.arange(row_count, dtype=jnp.int32)[:, None] * col_count + column
    wanted = (wanted * capacity + jnp.arange(capacity, dtype=jnp.int32)[None, :]).reshape(1, -1, 1)
    got_place = jnp.sum(jnp.where(near_slots == wanted, near_places + 1, 0), axis=2) - 1
    got_place = got_place.reshape(col_count, row_count, capacity).transpose(1, 0, 2)
    got_place = got_place.reshape(row_count, plane_slots, 1)
    at_place = got_place == jnp.arange(POSITIONS, dtype=jnp.int32)[None, None, :]

    def entries_of(table):
        entry = jnp.sum(jnp.where(at_place, table[:, None, :] + 1, 0), axis=2) - 1
        entry = jnp.where(got_place[..., 0] < 0, NOWHERE, entry)
        entry = entry.reshape(2, half, col_count, capacity)
        return entry.transpose(0, 2, 1, 3).reshape(-1)

    entry = jnp.stack([entries_of(first_at), entries_of(second_at)])
    slot = jnp.arange(row_count * plane_slots, dtype=jnp.int32)
    one, other = entry[:, :, None], entry[:, None, :]
    ahead = (other < one) | ((other == one) & (slot[None, None, :] < slot[None, :, None]))
    turn = jnp.sum(ahead.astype(jnp.int32), axis=2)
    tile_order = jnp.sum(
        jnp.where(turn[:, None, :] == slot[None, :, None], slot[None, None, :], 0), axis=2
    )
    below = entry[:, :, None] < jnp.arange(LIST_ENTRIES + 1, dtype=jnp.int32)[None, None, :]
    entry_bounds = jnp.einsum(
        "os,lse->loe",
        jnp.ones((8, slot.shape[0]), jnp.bfloat16),
        below.astype(jnp.bfloat16),
        preferred_element_type=jnp.float32,
    )[:, 0].astype(jnp.int32)
    def brought(at):
        since = jnp.where(at < FIRST_PAIR, at, at - FIRST_PAIR)
        return jnp.where((since < ALONE) & (at < LIST_ENTRIES), NOWHERE, at).reshape(-1)

    second_at = jnp.where(at_end == 1, second_at.reshape(-1), brought(second_at))
    first_at = brought(first_at)

    source, tile_order = lax.optimization_barrier((source, tile_order))
    chosen = sent_half(1)

    def through_lists(got, chosen, tiles, tile_target, tile_place, density):
        chosen, got = lax.optimization_barrier((chosen, got))
        got = [got, exchanged(chosen)]
        slabs = [passed_along(density, "col", -offset) for offset in range(STEPS)]
        slabs[0] = density
        groups = {
            0: [(1, 0), (0, 1), (0, 3)],
            1: [(0, 2), (0, 4), (1, 1), (1, 2), (1, 3), (1, 4)],
            3: [(0, 6), (0, 7), (0, 8), (0, 9), (1, 5), (1, 6)],
            6: [(0, 10), (0, 11), (0, 12), (1, 7), (1, 8), (1, 9)],
            8: [(1, 10), (1, 11), (1, 12)],
        }

        def sums_of(group, after):
            parts = 1 if max(chunk for _, chunk in group) * CHUNK < FIRST_PAIR else 2
            return listed_sums(got[:parts], tile_order, entry_bounds, group, after)

        chunks = chain_sums(sums_of, groups, slabs)
        place = jnp.stack([me, at_end]).astype(jnp.int32)
        common = (place, first_at, second_at, slabs, chunks)
        early, late = FIRST_DONE // CHUNK, FIRST_PAIR // CHUNK
        total = contracted(*common, range(half), (0, early), None, jnp.float32)
        end = LIST_ENTRIES // CHUNK
        return contracted(*common, range(half, row_count), (late, end), total, density.dtype)

    def round_the_ring(got, chosen, *args):
        return on_device_ring(*args)

    return lax.cond(
        fits,
        through_lists,
        round_the_ring,
        got[0],
        chosen,
        tiles,
        tile_target,
        tile_place,
        density,
    )


def solution(mesh):
    in_specs = (
        P(("row", "col"), None, None),
        P(("row", "col"), None),
        P(("row", "col")),
        P("col", "row"),
    )
    out_specs = P("col", "row")
    on_device = on_device_chain if mesh.shape["row"] == STEPS else on_device_ring
    return jax.shard_map(
        on_device, mesh=mesh, in_specs=in_specs, out_specs=out_specs, check_vma=False
    )
```
